256 devices in a mesh: band: 8 (over x, core), grid: 32 (over y, z).
Axes of the slice: x: 4, y: 4, z: 8, core: 2. Of those that a mesh axis runs over, the one named last changes fastest.
Arguments:
- bands: bfloat16 [16, 192, 192, 192], P('band', 'grid'), may hold values from -6 to 6
- plan: int32 [2, 8], replicated, may hold values from 0 to 7, as said below
Outputs:
- exchange_action: float32 [16, 192, 192, 192], P('band', 'grid')
The draws below stay inside these ranges and needn't reach their ends.
Inputs may be any that keep to these rules, and one draw needn't show every extreme that they name: plan[r, b] = b XOR m_r for a round mask m_r of 1 to 7, a different mask in each round.
All inputs are finite; a program needn't handle non-finite values.
Results may differ from the reference program's by a relative error of at most 0.009.
Values may be sent and summed in bfloat16 or wider, within the bound.
No kernel may reach another device: no remote copies, remote signals or barrier semaphores. Data moves between devices by JAX's collectives and lax.ppermute only.
A program may use at most 128 MiB of HBM per device.

```python
import math
import jax
import jax.numpy as jnp
from jax import lax

NG = 192
BPB = 2
ROUNDS = 2
NBANDS = 16
N_BAND = 8


def draw_plan(key, part):
    key = jax.random.fold_in(key, 7)
    masks = jax.random.permutation(key, N_BAND - 1)[:ROUNDS] + 1
    blocks = jnp.arange(N_BAND, dtype=jnp.int32)
    return jnp.bitwise_xor(blocks[None, :], masks[:, None].astype(jnp.int32)).astype(jnp.int32)


def levels(key, shape, cuts, smallest, largest):
    loudness, own = 1.0, jax.random.fold_in(key, 6)
    for axis_at, shards_of in cuts:
        draws = jnp.exp(jax.random.uniform(jax.random.fold_in(own, axis_at), (shards_of,), jnp.float32, smallest / len(cuts), largest / len(cuts)))
        loudness = loudness * jnp.repeat(draws, shape[axis_at] // shards_of).reshape([-1 if axis == axis_at else 1 for axis in range(len(shape))])
    return loudness


def centred(stream_key, dims, spread, reach, split=(), kind=jnp.bfloat16):
    array = jax.random.normal(stream_key, dims, jnp.float32) * spread
    if len(split) > 0:
        array = levels(stream_key, dims, split, -0.22, 0.18) * array
    return jnp.clip(array, min=-reach, max=reach).astype(kind)


def setup_inputs(seed: int = 0) -> dict:
    streams_of = jax.random.split(jax.random.key(seed), 3)
    return {
        "bands": centred(streams_of[0], (NBANDS, NG, NG, NG), 1.0, 6.0, ((0, 8), (1, 32))),
        "plan": draw_plan(jax.random.fold_in(streams_of[2], 71), 0),
    }


screening = 0.11
cell_edge = 46.9
mixing = 0.25

def folded(index_values, points):
    return jnp.where(index_values < points // 2, index_values, index_values - points)

def kernel_values(freq_x, freq_y, freq_z):
    squares = freq_x * freq_x + freq_y * freq_y + freq_z * freq_z
    factor = (2.0 * math.pi / cell_edge) ** 2 / (4.0 * screening ** 2)
    scaled = squares.astype(jnp.float32) * jnp.float32(factor)
    safe_value = jnp.where(squares == 0, jnp.float32(1.0), scaled)
    return jnp.where(squares == 0, jnp.float32(1.0), (1.0 - jnp.exp(-safe_value)) / safe_value)

def dft_tables(points):
    index_values = jnp.arange(points, dtype=jnp.int32)
    product = index_values[:, None] * index_values[None, :] % points
    angles = product.astype(jnp.float32) * jnp.float32(2.0 * math.pi / points)
    return (jnp.cos(angles).astype(jnp.bfloat16), jnp.sin(angles).astype(jnp.bfloat16))

def contract(pattern, left, right):
    return jnp.einsum(pattern, left.astype(jnp.float32), right.astype(jnp.float32), precision=lax.Precision.HIGHEST)

def spin(values_in, cosines, sines, pattern, direction):
    with_cos = contract(pattern, cosines, values_in)
    with_sin = contract(pattern, sines, values_in)
    half_len = values_in.shape[-1] // 2
    real_part = with_cos[..., :half_len] + direction * with_sin[..., half_len:]
    imag_part = with_cos[..., half_len:] - direction * with_sin[..., :half_len]
    return jnp.concatenate([real_part, imag_part], axis=-1)

def reference(bands, plan):
    blocks = bands.reshape(N_BAND, BPB, NG, NG, NG)
    cosines, sines = dft_tables(NG)
    forward_z = jnp.concatenate([cosines, -sines], axis=1)
    inverse_z = jnp.concatenate([cosines, -sines], axis=0)
    frequency = folded(jnp.arange(NG, dtype=jnp.int32), NG)
    kernel = kernel_values(frequency[:, None, None], frequency[None, :, None], frequency[None, None, :])
    norm_scale = 1.0 / jnp.sqrt(jnp.sum(kernel * kernel) / jnp.float32(NG ** 3))
    factor = norm_scale / jnp.float32(NG ** 3)
    kernel_both = jnp.concatenate([kernel, kernel], axis=-1)

    def potentials(density):
        first = contract('pxyz,zw->pxyw', density, forward_z).astype(jnp.bfloat16)
        along_y = spin(first, cosines, sines, 'uy,pxyw->pxuw', 1.0).astype(jnp.bfloat16)
        screened = (spin(along_y, cosines, sines, 'ux,pxyw->puyw', 1.0) * kernel_both).astype(jnp.bfloat16)
        back_x = spin(screened, cosines, sines, 'ux,pxyw->puyw', -1.0).astype(jnp.bfloat16)
        back_y = spin(back_x, cosines, sines, 'uy,pxyw->pxuw', -1.0).astype(jnp.bfloat16)
        return contract('pxyw,wz->pxyz', back_y, inverse_z) * factor
    accum = jnp.zeros((N_BAND, BPB, NG, NG, NG), jnp.float32)
    for round_index in range(ROUNDS):
        round_row = plan[round_index]

        def per_block(block_id):
            partner = round_row[block_id]
            partner_bands = blocks[partner]
            own_bands = blocks[block_id]
            is_high = block_id > partner
            chosen = jnp.where(is_high, partner_bands[::-1], partner_bands)
            density = (own_bands.astype(jnp.float32) * chosen.astype(jnp.float32)).astype(jnp.bfloat16)
            potential = potentials(density)
            mirror = (potential * own_bands.astype(jnp.float32)).astype(jnp.bfloat16)
            mirror = jnp.where(is_high, mirror[::-1], mirror)
            return (potential * chosen.astype(jnp.float32), mirror)
        own_terms, mirrors = lax.map(per_block, jnp.arange(N_BAND, dtype=jnp.int32))
        accum = accum + own_terms + mirrors[round_row].astype(jnp.float32)
    return (-mixing * accum).reshape(N_BAND * BPB, NG, NG, NG)
```

```python
import math

import jax
import jax.numpy as jnp
import numpy as np
from jax import lax
from jax.sharding import PartitionSpec as P

screening = 0.11
cell_edge = 46.9
mixing = 0.25
decay = (2.0 * math.pi / cell_edge) ** 2 / (4.0 * screening**2)


def folded(index_values, points):
    return jnp.where(index_values < points // 2, index_values, index_values - points)


def kernel_values(freq_x, freq_y, freq_z):
    squares = freq_x * freq_x + freq_y * freq_y + freq_z * freq_z
    scaled = squares.astype(jnp.float32) * jnp.float32(decay)
    safe_value = jnp.where(squares == 0, jnp.float32(1.0), scaled)
    return jnp.where(squares == 0, jnp.float32(1.0), (1.0 - jnp.exp(-safe_value)) / safe_value)


def host_factor(points):
    index_values = np.arange(points)
    freq = np.where(index_values < points // 2, index_values, index_values - points)
    sq = freq * freq
    squares = sq[:, None, None] + sq[None, :, None] + sq[None, None, :]
    values, counts = np.unique(squares, return_counts=True)
    scaled = np.where(values == 0, 1.0, values * decay)
    kernel = np.where(values == 0, 1.0, -np.expm1(-scaled) / scaled)
    power = float(np.sum(kernel * kernel * counts))
    return 1.0 / math.sqrt(power / points**3) / points**3


def host_tables(points):
    index_values = np.arange(points)
    product = index_values[:, None] * index_values[None, :] % points
    angles = product.astype(np.float64) * (2.0 * math.pi / points)
    return np.cos(angles).astype(jnp.bfloat16), np.sin(angles).astype(jnp.bfloat16)


def dot(pattern, left, right):
    return jnp.einsum(pattern, left, right, preferred_element_type=jnp.float32)


def spin(values_in, cosines, sines, pattern, direction):
    with_cos = dot(pattern, cosines, values_in)
    with_sin = dot(pattern, sines, values_in)
    half_len = values_in.shape[-1] // 2
    real_part = with_cos[..., :half_len] + direction * with_sin[..., half_len:]
    imag_part = with_cos[..., half_len:] - direction * with_sin[..., :half_len]
    return jnp.concatenate([real_part, imag_part], axis=-1)


def run_rounds(bands, masks):
    slab_cells = bands.shape[1]
    points = bands.shape[2]
    band_count = lax.axis_size("band")
    my_block = lax.axis_index("band")
    cos_np, sin_np = host_tables(points)
    cosines, sines = jnp.asarray(cos_np), jnp.asarray(sin_np)
    forward_z = jnp.asarray(
        np.concatenate(
            [np.concatenate([cos_np, -sin_np], 1), np.concatenate([sin_np, cos_np], 1)], 0
        )
    )
    inverse_z = jnp.asarray(
        np.concatenate(
            [np.concatenate([cos_np, sin_np], 1), np.concatenate([-sin_np, cos_np], 1)], 0
        )
    )
    factor = jnp.float32(host_factor(points))
    frequency = folded(jnp.arange(points, dtype=jnp.int32), points)
    column_ids = lax.axis_index("grid") * slab_cells + jnp.arange(slab_cells, dtype=jnp.int32)
    kernel_part = kernel_values(
        frequency[:, None, None],
        folded(column_ids, points)[None, :, None],
        frequency[None, None, :],
    )
    kernel_local = jnp.concatenate([kernel_part, kernel_part], axis=-1)

    def swap(values, mask):
        return lax.ppermute(values, "band", [(i, i ^ mask) for i in range(band_count)])

    def transform_in(density):
        packed = jnp.concatenate([density[0], density[1]], axis=-1)
        first = dot("xyz,zw->xyw", packed, forward_z).astype(jnp.bfloat16)
        return spin(first, cosines, sines, "uy,xyw->xuw", 1.0).astype(jnp.bfloat16)

    def screen_lines(spectrum):
        screened = (spin(spectrum, cosines, sines, "ux,xyw->uyw", 1.0) * kernel_local).astype(
            jnp.bfloat16
        )
        return spin(screened, cosines, sines, "ux,xyw->uyw", -1.0).astype(jnp.bfloat16)

    def transform_out(returned):
        back_y = spin(returned, cosines, sines, "uy,xyw->xuw", -1.0).astype(jnp.bfloat16)
        both = dot("xyw,wz->xyz", back_y, inverse_z) * factor
        return jnp.stack([both[..., :points], both[..., points:]])

    chosen_list = []
    spectra = []
    for mask in masks:
        is_high = my_block > jnp.bitwise_xor(my_block, mask)
        partner_bands = swap(bands, mask)
        chosen = jnp.where(is_high, partner_bands[::-1], partner_bands)
        density = (bands.astype(jnp.float32) * chosen.astype(jnp.float32)).astype(jnp.bfloat16)
        chosen_list.append((chosen, is_high))
        spectra.append(
            lax.all_to_all(transform_in(density), "grid", split_axis=1, concat_axis=0, tiled=True)
        )
    returned = [
        lax.all_to_all(screen_lines(spectrum), "grid", split_axis=0, concat_axis=1, tiled=True)
        for spectrum in spectra
    ]
    accum = jnp.zeros(bands.shape, jnp.float32)
    for mask, (chosen, is_high), lines in zip(masks, chosen_list, returned):
        potential = transform_out(lines)
        mirror = (potential * bands.astype(jnp.float32)).astype(jnp.bfloat16)
        mirror = swap(jnp.where(is_high, mirror[::-1], mirror), mask)
        accum = accum + potential * chosen.astype(jnp.float32) + mirror.astype(jnp.float32)
    return -mixing * accum


def per_device(bands, plan):
    band_count = lax.axis_size("band")
    pairs = [(i, j) for i in range(1, band_count) for j in range(i + 1, band_count)]
    low = jnp.minimum(plan[0, 0], plan[1, 0])
    high = jnp.maximum(plan[0, 0], plan[1, 0])
    skipped = (low - 1) * band_count - low * (low + 1) // 2 + 1
    branches = [lambda values, masks=masks: run_rounds(values, masks) for masks in pairs]
    return lax.switch(skipped + high - low - 1, branches, bands)


def solution(mesh):
    in_specs = (P("band", "grid", None, None), P())
    out_specs = P("band", "grid", None, None)
    return jax.shard_map(
        per_device, mesh=mesh, in_specs=in_specs, out_specs=out_specs, check_vma=False
    )
```

```python
import math

import jax
import jax.numpy as jnp
import numpy as np
from jax import lax
from jax.sharding import PartitionSpec as P

screening = 0.11
cell_edge = 46.9
mixing = 0.25
decay = (2.0 * math.pi / cell_edge) ** 2 / (4.0 * screening**2)


def folded(index_values, points):
    return jnp.where(index_values < points // 2, index_values, index_values - points)


def kernel_values(freq_x, freq_y, freq_z):
    squares = freq_x * freq_x + freq_y * freq_y + freq_z * freq_z
    scaled = squares.astype(jnp.float32) * jnp.float32(decay)
    safe_value = jnp.where(squares == 0, jnp.float32(1.0), scaled)
    return jnp.where(squares == 0, jnp.float32(1.0), (1.0 - jnp.exp(-safe_value)) / safe_value)


def host_factor(points):
    index_values = np.arange(points)
    freq = np.where(index_values < points // 2, index_values, index_values - points)
    sq = freq * freq
    squares = sq[:, None, None] + sq[None, :, None] + sq[None, None, :]
    values, counts = np.unique(squares, return_counts=True)
    scaled = np.where(values == 0, 1.0, values * decay)
    kernel = np.where(values == 0, 1.0, -np.expm1(-scaled) / scaled)
    power = float(np.sum(kernel * kernel * counts))
    return 1.0 / math.sqrt(power / points**3) / points**3


def host_tables(points):
    index_values = np.arange(points)
    product = index_values[:, None] * index_values[None, :] % points
    angles = product.astype(np.float64) * (2.0 * math.pi / points)
    return np.cos(angles).astype(jnp.bfloat16), np.sin(angles).astype(jnp.bfloat16)


def dot(pattern, left, right):
    return jnp.einsum(pattern, left, right, preferred_element_type=jnp.float32)


def spin(values_in, cosines, sines, pattern, direction):
    with_cos = dot(pattern, cosines, values_in)
    with_sin = dot(pattern, sines, values_in)
    half_len = values_in.shape[-1] // 2
    real_part = with_cos[..., :half_len] + direction * with_sin[..., half_len:]
    imag_part = with_cos[..., half_len:] - direction * with_sin[..., :half_len]
    return jnp.concatenate([real_part, imag_part], axis=-1)


def per_device(bands, plan):
    slab_cells = bands.shape[1]
    points = bands.shape[2]
    band_count = lax.axis_size("band")
    my_block = lax.axis_index("band")
    cos_np, sin_np = host_tables(points)
    cosines, sines = jnp.asarray(cos_np), jnp.asarray(sin_np)
    forward_z = jnp.asarray(
        np.concatenate(
            [np.concatenate([cos_np, -sin_np], 1), np.concatenate([sin_np, cos_np], 1)], 0
        )
    )
    inverse_z = jnp.asarray(
        np.concatenate(
            [np.concatenate([cos_np, sin_np], 1), np.concatenate([-sin_np, cos_np], 1)], 0
        )
    )
    factor = jnp.float32(host_factor(points))
    frequency = folded(jnp.arange(points, dtype=jnp.int32), points)
    column_ids = lax.axis_index("grid") * slab_cells + jnp.arange(slab_cells, dtype=jnp.int32)
    kernel_part = kernel_values(
        frequency[:, None, None],
        folded(column_ids, points)[None, :, None],
        frequency[None, None, :],
    )
    kernel_local = jnp.concatenate([kernel_part, kernel_part], axis=-1)

    def swap(values, mask):
        return lax.ppermute(values, "band", [(i, i ^ mask) for i in range(band_count)])

    def transform_in(density):
        packed = jnp.concatenate([density[0], density[1]], axis=-1)
        first = dot("xyz,zw->xyw", packed, forward_z).astype(jnp.bfloat16)
        return spin(first, cosines, sines, "uy,xyw->xuw", 1.0).astype(jnp.bfloat16)

    def screen_lines(spectrum):
        screened = (spin(spectrum, cosines, sines, "ux,xyw->uyw", 1.0) * kernel_local).astype(
            jnp.bfloat16
        )
        return spin(screened, cosines, sines, "ux,xyw->uyw", -1.0).astype(jnp.bfloat16)

    def transform_out(returned):
        back_y = spin(returned, cosines, sines, "uy,xyw->xuw", -1.0).astype(jnp.bfloat16)
        both = dot("xyw,wz->xyz", back_y, inverse_z) * factor
        return jnp.stack([both[..., :points], both[..., points:]])

    def exchange(values, mask):
        branches = [lambda v, k=k: swap(v, k) for k in range(1, band_count)]
        return lax.switch(mask - 1, branches, values)

    def densities(mask, partner_bands):
        is_high = my_block > jnp.bitwise_xor(my_block, mask)
        chosen = jnp.where(is_high, partner_bands[::-1], partner_bands)
        density = (bands.astype(jnp.float32) * chosen.astype(jnp.float32)).astype(jnp.bfloat16)
        return chosen, density

    def to_lines(spectrum):
        return lax.all_to_all(spectrum, "grid", split_axis=1, concat_axis=0, tiled=True)

    def to_planes(lines):
        return lax.all_to_all(lines, "grid", split_axis=0, concat_axis=1, tiled=True)

    def finish(mask, lines, chosen):
        is_high = my_block > jnp.bitwise_xor(my_block, mask)
        potential = transform_out(lines)
        mirror = (potential * bands.astype(jnp.float32)).astype(jnp.bfloat16)
        mirror = jnp.where(is_high, mirror[::-1], mirror)
        return potential * chosen.astype(jnp.float32), mirror

    together = lax.optimization_barrier
    mask_a, mask_b = plan[0, 0], plan[1, 0]
    chosen_a, density_a = densities(mask_a, exchange(bands, mask_a))
    planes_a, bands_b = together((transform_in(density_a), bands))
    lines_a = to_lines(planes_a)
    chosen_b, density_b = densities(mask_b, exchange(bands_b, mask_b))
    lines_a, planes_b = together((lines_a, transform_in(density_b)))
    lines_b = to_lines(planes_b)
    lines_b, screened_a = together((lines_b, screen_lines(lines_a)))
    back_a = to_planes(screened_a)
    back_a, screened_b = together((back_a, screen_lines(lines_b)))
    back_b = to_planes(screened_b)
    own_a, mirror_a = finish(mask_a, back_a, chosen_a)
    back_b, own_a, got_a = together((back_b, own_a, exchange(mirror_a, mask_a)))
    own_b, mirror_b = finish(mask_b, back_b, chosen_b)
    got_b = exchange(mirror_b, mask_b)
    return -mixing * (own_a + own_b + got_a.astype(jnp.float32) + got_b.astype(jnp.float32))


def solution(mesh):
    in_specs = (P("band", "grid", None, None), P())
    out_specs = P("band", "grid", None, None)
    return jax.shard_map(
        per_device, mesh=mesh, in_specs=in_specs, out_specs=out_specs, check_vma=False
    )
```

```python
import math

import jax
import jax.numpy as jnp
import numpy as np
from jax import lax
from jax.sharding import PartitionSpec as P

screening = 0.11
cell_edge = 46.9
mixing = 0.25
decay = (2.0 * math.pi / cell_edge) ** 2 / (4.0 * screening**2)


def folded(index_values, points):
    return jnp.where(index_values < points // 2, index_values, index_values - points)


def kernel_values(freq_x, freq_y, freq_z):
    squares = freq_x * freq_x + freq_y * freq_y + freq_z * freq_z
    scaled = squares.astype(jnp.float32) * jnp.float32(decay)
    safe_value = jnp.where(squares == 0, jnp.float32(1.0), scaled)
    return jnp.where(squares == 0, jnp.float32(1.0), (1.0 - jnp.exp(-safe_value)) / safe_value)


def host_factor(points):
    index_values = np.arange(points)
    freq = np.where(index_values < points // 2, index_values, index_values - points)
    sq = freq * freq
    squares = sq[:, None, None] + sq[None, :, None] + sq[None, None, :]
    values, counts = np.unique(squares, return_counts=True)
    scaled = np.where(values == 0, 1.0, values * decay)
    kernel = np.where(values == 0, 1.0, -np.expm1(-scaled) / scaled)
    power = float(np.sum(kernel * kernel * counts))
    return 1.0 / math.sqrt(power / points**3) / points**3


def host_tables(points):
    index_values = np.arange(points)
    product = index_values[:, None] * index_values[None, :] % points
    angles = product.astype(np.float64) * (2.0 * math.pi / points)
    return np.cos(angles).astype(jnp.bfloat16), np.sin(angles).astype(jnp.bfloat16)


def dot(pattern, left, right):
    return jnp.einsum(pattern, left, right, preferred_element_type=jnp.float32)


def spin(values_in, cosines, sines, pattern, direction):
    with_cos = dot(pattern, cosines, values_in)
    with_sin = dot(pattern, sines, values_in)
    half_len = values_in.shape[-1] // 2
    real_part = with_cos[..., :half_len] + direction * with_sin[..., half_len:]
    imag_part = with_cos[..., half_len:] - direction * with_sin[..., :half_len]
    return jnp.concatenate([real_part, imag_part], axis=-1)


def per_device(bands, plan):
    slab_cells = bands.shape[1]
    points = bands.shape[2]
    band_count = lax.axis_size("band")
    my_block = lax.axis_index("band")
    cos_np, sin_np = host_tables(points)
    cosines, sines = jnp.asarray(cos_np), jnp.asarray(sin_np)
    forward_z = jnp.asarray(
        np.concatenate(
            [np.concatenate([cos_np, -sin_np], 1), np.concatenate([sin_np, cos_np], 1)], 0
        )
    )
    inverse_z = jnp.asarray(
        np.concatenate(
            [np.concatenate([cos_np, sin_np], 1), np.concatenate([-sin_np, cos_np], 1)], 0
        )
    )
    factor = jnp.float32(host_factor(points))
    frequency = folded(jnp.arange(points, dtype=jnp.int32), points)
    column_ids = lax.axis_index("grid") * slab_cells + jnp.arange(slab_cells, dtype=jnp.int32)
    kernel_part = kernel_values(
        frequency[:, None, None],
        folded(column_ids, points)[None, :, None],
        frequency[None, None, :],
    )
    kernel_local = jnp.concatenate([kernel_part, kernel_part], axis=-1)

    def swap(values, mask):
        return lax.ppermute(values, "band", [(i, i ^ mask) for i in range(band_count)])

    low = jnp.minimum(plan[0, 0], plan[1, 0])
    high = jnp.maximum(plan[0, 0], plan[1, 0])
    chip_low, chip_high = low // 2, high // 2
    chip_masks = range(1, band_count // 2)
    one_chip = chip_low == chip_high
    single = jnp.logical_or(chip_low == 0, one_chip)
    pairs = [(i, j) for i in chip_masks for j in chip_masks if i < j]
    pair_index = sum(
        jnp.where(jnp.logical_and(chip_low == i, chip_high == j), n + len(chip_masks), 0)
        for n, (i, j) in enumerate(pairs)
    )
    branch_index = jnp.where(single, chip_high - 1, pair_index)
    fetch_index = jnp.where(one_chip, chip_high - 1 + len(chip_masks) + len(pairs), branch_index)
    is_high = [my_block > jnp.bitwise_xor(my_block, mask) for mask in (low, high)]
    crossed = [mask % 2 == 1 for mask in (low, high)]

    def exchange_branches():
        singles = [lambda u, v, m=m: (u, swap(v, 2 * m)) for m in chip_masks]
        doubles = [lambda u, v, m=m: (swap(u, 2 * m[0]), swap(v, 2 * m[1])) for m in pairs]
        return singles + doubles

    def same_chip(mask):
        def branch(u, v):
            got = swap(v, 2 * mask)
            return swap(got, 1), got

        return branch

    sibling = swap(bands, 1)

    def fetch(values, other, band):
        sent = []
        for mask, flag, cross in zip((low, high), is_high, crossed):
            first = jnp.logical_xor(flag, mask == 1)
            own = jnp.where(first, values[band], values[1 - band])
            sent.append(jnp.where(cross, jnp.where(first, other[band], other[1 - band]), own))
        branches = exchange_branches() + [same_chip(m) for m in chip_masks]
        return lax.switch(fetch_index, branches, *sent)

    def give_back(mirrors):
        sent = [jnp.where(c, swap(m, 1), m) for c, m in zip(crossed, mirrors)]
        total = (sent[0].astype(jnp.float32) + sent[1].astype(jnp.float32)).astype(jnp.bfloat16)
        first = jnp.where(one_chip, jnp.zeros_like(total), sent[0])
        second = jnp.where(one_chip, total, sent[1])
        return lax.switch(branch_index, exchange_branches(), first, second)

    def transform_in(band, partners):
        densities = [bands[band].astype(jnp.float32) * c.astype(jnp.float32) for c in partners]
        packed = jnp.concatenate(densities, axis=-1).astype(jnp.bfloat16)
        first = dot("xyz,zw->xyw", packed, forward_z).astype(jnp.bfloat16)
        spectrum = spin(first, cosines, sines, "uy,xyw->uxw", 1.0).astype(jnp.bfloat16)
        return spectrum.reshape(points, slab_cells // 2, 2, 2 * points)

    def send(values):
        return lax.all_to_all(values, "grid", split_axis=0, concat_axis=0, tiled=True)

    def screen_lines(received):
        lines = received.reshape(points // slab_cells, slab_cells, slab_cells, 2 * points)
        lines = lines.transpose(0, 2, 1, 3).reshape(points, slab_cells, 2 * points)
        screened = (spin(lines, cosines, sines, "ux,xyw->uyw", 1.0) * kernel_local).astype(
            jnp.bfloat16
        )
        back = spin(screened, cosines, sines, "ux,xyw->uyw", -1.0).astype(jnp.bfloat16)
        return back.reshape(points, slab_cells // 2, 2, 2 * points)

    def transform_out(received):
        lines = received.reshape(points // slab_cells, slab_cells, slab_cells, 2 * points)
        lines = lines.transpose(1, 0, 2, 3).reshape(slab_cells, points, 2 * points)
        back_y = spin(lines, cosines, sines, "uy,xyw->xuw", -1.0).astype(jnp.bfloat16)
        both = dot("xyw,wz->xyz", back_y, inverse_z) * factor
        return both[..., :points], both[..., points:]

    def finish(band, partners, received):
        own = jnp.zeros(bands.shape[1:], jnp.float32)
        mirrors = []
        for potential, partner in zip(transform_out(received), partners):
            own = own + potential * partner.astype(jnp.float32)
            mirrors.append((potential * bands[band].astype(jnp.float32)).astype(jnp.bfloat16))
        return own, mirrors

    def place(band, mirrors):
        sums = []
        for target in (0, 1):
            total = 0.0
            for flag, mirror in zip(is_high, mirrors):
                here = flag if band == target else jnp.logical_not(flag)
                total = total + jnp.where(here, mirror.astype(jnp.float32), 0.0)
            sums.append(total)
        return sums

    together = lax.optimization_barrier
    partners_a = fetch(bands, sibling, 0)
    planes_a, bands_b, sibling_b = together((transform_in(0, partners_a), bands, sibling))
    lines_a = send(planes_a)
    partners_b = fetch(bands_b, sibling_b, 1)
    lines_a, planes_b = together((lines_a, transform_in(1, partners_b)))
    lines_b = send(planes_b)
    lines_b, screened_a = together((lines_b, screen_lines(lines_a)))
    back_a = send(screened_a)
    back_a, screened_b = together((back_a, screen_lines(lines_b)))
    back_b = send(screened_b)
    own_a, mirrors_a = finish(0, partners_a, back_a)
    got_a = place(0, give_back(mirrors_a))
    part_a = -mixing * (own_a + got_a[0])
    back_b, part_a, part_b = together((back_b, part_a, -mixing * got_a[1]))
    own_b, mirrors_b = finish(1, partners_b, back_b)
    part_b = part_b - mixing * own_b
    mirrors_b, part_b = together((mirrors_b, part_b))
    got_b = place(1, give_back(mirrors_b))
    return jnp.stack([part_a - mixing * got_b[0], part_b - mixing * got_b[1]])


def solution(mesh):
    in_specs = (P("band", "grid", None, None), P())
    out_specs = P("band", "grid", None, None)
    return jax.shard_map(
        per_device, mesh=mesh, in_specs=in_specs, out_specs=out_specs, check_vma=False
    )
```

```python
import math

import jax
import jax.numpy as jnp
import numpy as np
from jax import lax
from jax.experimental import pallas as pl
from jax.experimental.pallas import tpu as pltpu
from jax.sharding import PartitionSpec as P

screening = 0.11
cell_edge = 46.9
mixing = 0.25
decay = (2.0 * math.pi / cell_edge) ** 2 / (4.0 * screening**2)


def folded(index_values, points):
    return jnp.where(index_values < points // 2, index_values, index_values - points)


def kernel_values(freq_x, freq_y, freq_z):
    squares = freq_x * freq_x + freq_y * freq_y + freq_z * freq_z
    scaled = squares.astype(jnp.float32) * jnp.float32(decay)
    safe_value = jnp.where(squares == 0, jnp.float32(1.0), scaled)
    return jnp.where(squares == 0, jnp.float32(1.0), (1.0 - jnp.exp(-safe_value)) / safe_value)


def host_factor(points):
    index_values = np.arange(points)
    freq = np.where(index_values < points // 2, index_values, index_values - points)
    sq = freq * freq
    squares = sq[:, None, None] + sq[None, :, None] + sq[None, None, :]
    values, counts = np.unique(squares, return_counts=True)
    scaled = np.where(values == 0, 1.0, values * decay)
    kernel = np.where(values == 0, 1.0, -np.expm1(-scaled) / scaled)
    power = float(np.sum(kernel * kernel * counts))
    return 1.0 / math.sqrt(power / points**3) / points**3


def host_tables(points):
    index_values = np.arange(points)
    product = index_values[:, None] * index_values[None, :] % points
    angles = product.astype(np.float64) * (2.0 * math.pi / points)
    return np.cos(angles).astype(jnp.bfloat16), np.sin(angles).astype(jnp.bfloat16)


def lane_order(points):
    whole = points // 128 * 128
    real, imag = np.arange(points), points + np.arange(points)
    return np.concatenate([real[:whole], imag[:whole], real[whole:], imag[whole:]])


def device_tables(points, slab):
    cos_np, sin_np = host_tables(points)
    order = lane_order(points)
    forward = np.concatenate(
        [np.concatenate([cos_np, -sin_np], 1), np.concatenate([sin_np, cos_np], 1)], 0
    )[:, order]
    backward = np.concatenate(
        [np.concatenate([cos_np, sin_np], 1), np.concatenate([-sin_np, cos_np], 1)], 0
    )[order]
    eye = np.eye(2, dtype=cos_np.dtype)
    double = [
        (t[:, None, None, :] * eye[None, :, :, None]).reshape(2 * points, 2 * points)
        for t in (cos_np, sin_np)
    ]
    lines = np.arange(points).reshape(points // slab, slab // 2, 2).transpose(1, 0, 2).reshape(-1)
    single = [t[:, lines] for t in (cos_np, sin_np)]
    return forward, backward, np.stack(double), np.stack(single)


def matmul(left, right):
    return jnp.dot(left, right, preferred_element_type=jnp.float32)


def spin(tables, values, direction):
    with_cos = matmul(tables[0], values)
    with_sin = matmul(tables[1], values)
    whole = values.shape[1] // 256 * 128
    rest = values.shape[1] - 2 * whole
    real = with_cos[:, :whole] + direction * with_sin[:, whole : 2 * whole]
    imag = with_cos[:, whole : 2 * whole] - direction * with_sin[:, :whole]
    turned = pltpu.roll(with_sin[:, 2 * whole :], rest // 2, 1)
    lanes = lax.broadcasted_iota(jnp.int32, turned.shape, 1)
    turned = jnp.where(lanes < rest // 2, direction * turned, -direction * turned)
    return real, imag, with_cos[:, 2 * whole :] + turned


def joined(parts):
    return jnp.concatenate([part.astype(jnp.bfloat16) for part in parts], axis=1)


def forward_kernel(own, low, high, forward, double, out):
    points = own.shape[-1]
    rows = 2 * points

    def density(partner):
        product = own[0].astype(jnp.float32) * partner[...].astype(jnp.float32)
        return product.astype(jnp.bfloat16).reshape(rows, points)

    first = matmul(density(low), forward[:points]) + matmul(density(high), forward[points:])
    spectrum = joined(spin(double, first.astype(jnp.bfloat16), 1.0))
    out[:, 0] = spectrum.reshape(points, 2, rows)


def screen_kernel(lines, kernel, single, double, out):
    points = out.shape[0]
    whole = points // 128 * 128
    screened = []
    for member in range(2):
        gathered = jnp.concatenate(
            [lines[:, member, pair].reshape(-1, 2 * points) for pair in range(lines.shape[2])], 0
        )
        real, imag, rest = spin(single, gathered, 1.0)
        near, far = kernel[member, :, :whole], kernel[member, :, whole:]
        screened.append(joined([real * near, imag * near, rest * far]))
    back = joined(spin(double, jnp.concatenate(screened, 0), -1.0))
    out[:, 0] = back.reshape(points, 2, 2 * points)


def backward_kernel(factor, lines, band, low, high, single, backward, own, to_low, to_high):
    points = band.shape[-1]
    for member in range(2):
        gathered = jnp.concatenate(
            [lines[:, member, pair].reshape(-1, 2 * points) for pair in range(lines.shape[2])], 0
        )
        back = joined(spin(single, gathered, -1.0))
        mine = band[0, member].astype(jnp.float32)
        total = jnp.zeros((points, points), jnp.float32)
        for partner, mirror, start in ((low, to_low, 0), (high, to_high, points)):
            potential = matmul(back, backward[:, start : start + points]) * factor
            mirror[member] = (potential * mine).astype(jnp.bfloat16)
            total = total + potential * partner[member].astype(jnp.float32)
        own[member] = -mixing * total


def combine_kernel(flags, own_a, own_b, a_low, a_high, b_low, b_high, out):
    for target, own in enumerate((own_a, own_b)):
        total = own[...]
        for n, (from_a, from_b) in enumerate(((a_low, b_low), (a_high, b_high))):
            kept = flags[n] == 1 - target
            got = jnp.where(kept, from_a[...].astype(jnp.float32), from_b[...].astype(jnp.float32))
            total = total - mixing * got
        out[target] = total


def whole_spec(array):
    rank = len(array.shape)
    return pl.BlockSpec(array.shape, lambda s: (0,) * rank)


def planes_spec(points):
    return pl.BlockSpec((2, points, points), lambda s: (s, 0, 0))


def band_spec(band, points):
    return pl.BlockSpec((1, 2, points, points), lambda s: (band, s, 0, 0))


def lines_spec(points, slab):
    block = (points // slab, 2, slab // 2, 2, 2 * points)
    return pl.BlockSpec(block, lambda s: (0, s, 0, 0, 0))


def payload_spec(points):
    return pl.BlockSpec((points, 1, 2, 2 * points), lambda s: (0, s, 0, 0))


params = pltpu.CompilerParams(vmem_limit_bytes=48 * 1024 * 1024)


def per_device(bands, plan):
    slab_cells = bands.shape[1]
    points = bands.shape[2]
    band_count = lax.axis_size("band")
    my_block = lax.axis_index("band")
    forward, backward, double, single = [
        jnp.asarray(table) for table in device_tables(points, slab_cells)
    ]
    steps = slab_cells // 2
    payload = jax.ShapeDtypeStruct((points, steps, 2, 2 * points), jnp.bfloat16)
    received_shape = (points // slab_cells, slab_cells, steps, 2, 2 * points)
    factor = host_factor(points)
    frequency = folded(jnp.arange(points, dtype=jnp.int32), points)
    column_ids = lax.axis_index("grid") * slab_cells + jnp.arange(slab_cells, dtype=jnp.int32)
    kernel_part = kernel_values(
        folded(column_ids, points)[:, None, None],
        frequency[None, :, None],
        jnp.concatenate([frequency, frequency[points // 128 * 128 :]])[None, None, :],
    )

    def swap(values, mask):
        return lax.ppermute(values, "band", [(i, i ^ mask) for i in range(band_count)])

    low = jnp.minimum(plan[0, 0], plan[1, 0])
    high = jnp.maximum(plan[0, 0], plan[1, 0])
    chip_low, chip_high = low // 2, high // 2
    chip_masks = range(1, band_count // 2)
    one_chip = chip_low == chip_high
    lone = jnp.logical_or(chip_low == 0, one_chip)
    pairs = [(i, j) for i in chip_masks for j in chip_masks if i < j]
    pair_index = sum(
        jnp.where(jnp.logical_and(chip_low == i, chip_high == j), n + len(chip_masks), 0)
        for n, (i, j) in enumerate(pairs)
    )
    branch_index = jnp.where(lone, chip_high - 1, pair_index)
    fetch_index = jnp.where(one_chip, chip_high - 1 + len(chip_masks) + len(pairs), branch_index)
    is_high = [my_block > jnp.bitwise_xor(my_block, mask) for mask in (low, high)]
    crossed = [mask % 2 == 1 for mask in (low, high)]

    def exchange_branches():
        singles = [lambda u, v, m=m: (u, swap(v, 2 * m)) for m in chip_masks]
        doubles = [lambda u, v, m=m: (swap(u, 2 * m[0]), swap(v, 2 * m[1])) for m in pairs]
        return singles + doubles

    def same_chip(mask):
        def branch(u, v):
            got = swap(v, 2 * mask)
            return swap(got, 1), got

        return branch

    sibling = swap(bands, 1)

    def fetch(values, other, band):
        sent = []
        for mask, flag, cross in zip((low, high), is_high, crossed):
            first = jnp.logical_xor(flag, mask == 1)
            own = jnp.where(first, values[band], values[1 - band])
            sent.append(jnp.where(cross, jnp.where(first, other[band], other[1 - band]), own))
        branches = exchange_branches() + [same_chip(m) for m in chip_masks]
        return lax.switch(fetch_index, branches, *sent)

    def give_back(mirrors):
        sent = [jnp.where(c, swap(m, 1), m) for c, m in zip(crossed, mirrors)]
        total = (sent[0].astype(jnp.float32) + sent[1].astype(jnp.float32)).astype(jnp.bfloat16)
        first = jnp.where(one_chip, jnp.zeros_like(total), sent[0])
        second = jnp.where(one_chip, total, sent[1])
        return lax.switch(branch_index, exchange_branches(), first, second)

    def transform_in(band, partners):
        return pl.pallas_call(
            forward_kernel,
            grid=(steps,),
            in_specs=[
                band_spec(band, points),
                planes_spec(points),
                planes_spec(points),
                whole_spec(forward),
                whole_spec(double),
            ],
            out_specs=payload_spec(points),
            out_shape=payload,
            compiler_params=params,
        )(bands, *partners, forward, double)

    def send(values):
        return lax.all_to_all(values, "grid", split_axis=0, concat_axis=0, tiled=True)

    def screen_lines(received):
        return pl.pallas_call(
            screen_kernel,
            grid=(steps,),
            in_specs=[
                lines_spec(points, slab_cells),
                pl.BlockSpec((2,) + kernel_part.shape[1:], lambda s: (s, 0, 0)),
                whole_spec(single),
                whole_spec(double),
            ],
            out_specs=payload_spec(points),
            out_shape=payload,
            compiler_params=params,
        )(received.reshape(received_shape), kernel_part, single, double)

    def finish(band, partners, received):
        plane = (slab_cells, points, points)
        return pl.pallas_call(
            lambda *refs: backward_kernel(factor, *refs),
            grid=(steps,),
            in_specs=[
                lines_spec(points, slab_cells),
                band_spec(band, points),
                planes_spec(points),
                planes_spec(points),
                whole_spec(single),
                whole_spec(backward),
            ],
            out_specs=[planes_spec(points)] * 3,
            out_shape=[
                jax.ShapeDtypeStruct(plane, jnp.float32),
                jax.ShapeDtypeStruct(plane, jnp.bfloat16),
                jax.ShapeDtypeStruct(plane, jnp.bfloat16),
            ],
            compiler_params=params,
        )(received.reshape(received_shape), bands, *partners, single, backward)

    def combine(own_a, own_b, got_a, got_b):
        flags = jnp.stack(is_high).astype(jnp.int32)
        return pl.pallas_call(
            combine_kernel,
            grid=(steps,),
            in_specs=[pl.BlockSpec(memory_space=pltpu.SMEM)] + [planes_spec(points)] * 6,
            out_specs=pl.BlockSpec((2, 2, points, points), lambda s: (0, s, 0, 0)),
            out_shape=jax.ShapeDtypeStruct(bands.shape, jnp.float32),
            compiler_params=params,
        )(flags, own_a, own_b, *got_a, *got_b)

    together = lax.optimization_barrier
    partners_a = fetch(bands, sibling, 0)
    planes_a, bands_b, sibling_b = together((transform_in(0, partners_a), bands, sibling))
    lines_a = send(planes_a)
    partners_b = fetch(bands_b, sibling_b, 1)
    lines_a, planes_b = together((lines_a, transform_in(1, partners_b)))
    lines_b = send(planes_b)
    lines_b, screened_a = together((lines_b, screen_lines(lines_a)))
    back_a = send(screened_a)
    back_a, screened_b = together((back_a, screen_lines(lines_b)))
    back_b = send(screened_b)
    own_a, *mirrors_a = finish(0, partners_a, back_a)
    got_a = give_back(mirrors_a)
    back_b, own_a, got_a = together((back_b, own_a, got_a))
    own_b, *mirrors_b = finish(1, partners_b, back_b)
    got_b = give_back(mirrors_b)
    return combine(own_a, own_b, got_a, got_b)


def solution(mesh):
    in_specs = (P("band", "grid", None, None), P())
    out_specs = P("band", "grid", None, None)
    return jax.shard_map(
        per_device, mesh=mesh, in_specs=in_specs, out_specs=out_specs, check_vma=False
    )
```

```python
import math

import jax
import jax.numpy as jnp
import numpy as np
from jax import lax
from jax.experimental import pallas as pl
from jax.experimental.pallas import tpu as pltpu
from jax.sharding import PartitionSpec as P

screening = 0.11
cell_edge = 46.9
mixing = 0.25
decay = (2.0 * math.pi / cell_edge) ** 2 / (4.0 * screening**2)


def folded(index_values, points):
    return jnp.where(index_values < points // 2, index_values, index_values - points)


def kernel_values(freq_x, freq_y, freq_z):
    squares = freq_x * freq_x + freq_y * freq_y + freq_z * freq_z
    scaled = squares.astype(jnp.float32) * jnp.float32(decay)
    safe_value = jnp.where(squares == 0, jnp.float32(1.0), scaled)
    return jnp.where(squares == 0, jnp.float32(1.0), (1.0 - jnp.exp(-safe_value)) / safe_value)


def host_factor(points):
    index_values = np.arange(points)
    freq = np.where(index_values < points // 2, index_values, index_values - points)
    sq = freq * freq
    squares = sq[:, None, None] + sq[None, :, None] + sq[None, None, :]
    values, counts = np.unique(squares, return_counts=True)
    scaled = np.where(values == 0, 1.0, values * decay)
    kernel = np.where(values == 0, 1.0, -np.expm1(-scaled) / scaled)
    power = float(np.sum(kernel * kernel * counts))
    return 1.0 / math.sqrt(power / points**3) / points**3


def host_tables(points):
    index_values = np.arange(points)
    product = index_values[:, None] * index_values[None, :] % points
    angles = product.astype(np.float64) * (2.0 * math.pi / points)
    return np.cos(angles).astype(jnp.bfloat16), np.sin(angles).astype(jnp.bfloat16)


def lane_order(points):
    whole = points // 128 * 128
    real, imag = np.arange(points), points + np.arange(points)
    return np.concatenate([real[:whole], imag[:whole], real[whole:], imag[whole:]])


def device_tables(points, slab):
    cos_np, sin_np = host_tables(points)
    order = lane_order(points)
    forward = np.concatenate(
        [np.concatenate([cos_np, -sin_np], 1), np.concatenate([sin_np, cos_np], 1)], 0
    )[:, order]
    backward = np.concatenate(
        [np.concatenate([cos_np, sin_np], 1), np.concatenate([-sin_np, cos_np], 1)], 0
    )[order]
    lines = np.arange(points).reshape(points // slab, slab // 2, 2).transpose(1, 0, 2).reshape(-1)
    single = [t[:, lines] for t in (cos_np, sin_np)]
    eye = np.eye(2, dtype=cos_np.dtype)
    slabs = np.arange(points).reshape(points // slab, slab).transpose(1, 0).reshape(-1)
    gather = [
        (t[:, slabs][None, :, :, None] * eye[:, None, None, :]).reshape(2 * points, 2 * points)
        for t in (cos_np, sin_np)
    ]
    scatter = [
        (t[:, None, None, :] * eye[None, :, :, None]).reshape(2 * points, 2 * points)
        for t in (cos_np, sin_np)
    ]
    plain = [cos_np, sin_np]
    return [forward, backward] + [np.stack(t) for t in (plain, single, gather, scatter)]


def matmul(left, right):
    return jnp.dot(left, right, preferred_element_type=jnp.float32)


def spin(tables, values, direction):
    with_cos = matmul(tables[0], values)
    with_sin = matmul(tables[1], values)
    whole = values.shape[1] // 256 * 128
    rest = values.shape[1] - 2 * whole
    real = with_cos[:, :whole] + direction * with_sin[:, whole : 2 * whole]
    imag = with_cos[:, whole : 2 * whole] - direction * with_sin[:, :whole]
    turned = pltpu.roll(with_sin[:, 2 * whole :], rest // 2, 1)
    lanes = lax.broadcasted_iota(jnp.int32, turned.shape, 1)
    turned = jnp.where(lanes < rest // 2, direction * turned, -direction * turned)
    return real, imag, with_cos[:, 2 * whole :] + turned


def joined(parts):
    return jnp.concatenate([part.astype(jnp.bfloat16) for part in parts], axis=1)


def packed(plane):
    whole = plane.shape[1] // 128 * 128
    half = plane.shape[0] // 2
    rest = jnp.concatenate([plane[:half, whole:], plane[half:, whole:]], axis=1)
    return jnp.concatenate([plane[:, :whole], rest], axis=0)


def unpacked(plane):
    rows = plane.shape[0] * 2 // 3
    half = plane.shape[1] // 2
    rest = jnp.concatenate([plane[rows:, :half], plane[rows:, half:]], axis=0)
    return jnp.concatenate([plane[:rows], rest], axis=1)


def pack_kernel(flags, own_low, other_low, own_high, other_high, low, high):
    for n, (own, other, out) in enumerate(
        ((own_low, other_low, low), (own_high, other_high, high))
    ):
        for member in range(out.shape[0]):
            mine = own[0, member].astype(jnp.float32)
            theirs = other[0, member].astype(jnp.float32)
            plane = jnp.where(flags[2 + n] == 1, theirs, mine)
            out[member] = packed(plane).astype(jnp.bfloat16)


def forward_kernel(own, low, high, forward, plain, out):
    points = own.shape[-1]
    for member in range(own.shape[1]):
        mine = own[0, member].astype(jnp.float32)

        def density(partner):
            return (mine * unpacked(partner[member].astype(jnp.float32))).astype(jnp.bfloat16)

        first = matmul(density(low), forward[:points]) + matmul(density(high), forward[points:])
        spectrum = joined(spin(plain, first.astype(jnp.bfloat16), 1.0))
        out[:, member] = spectrum.reshape(points // 2, 2, 2 * points)


def screen_kernel(lines, kernel, gather, scatter, out):
    points = out.shape[0]
    whole = points // 128 * 128
    gathered = jnp.concatenate(
        [lines[:, 0, plane].reshape(-1, 2 * points) for plane in range(lines.shape[2])], 0
    )
    real, imag, rest = spin(gather, gathered, 1.0)
    near = kernel[:, :, :whole].reshape(2 * points, whole)
    far = kernel[:, :, whole:].reshape(2 * points, whole)
    screened = joined([real * near, imag * near, rest * far])
    back = joined(spin(scatter, screened, -1.0))
    out[:, 0] = back.reshape(points, 2, 2 * points)


def backward_kernel(factor, lines, band, low, high, single, backward, own, to_low, to_high):
    points = band.shape[-1]
    for member in range(2):
        gathered = jnp.concatenate(
            [lines[:, member, pair].reshape(-1, 2 * points) for pair in range(lines.shape[2])], 0
        )
        back = joined(spin(single, gathered, -1.0))
        mine = band[0, member].astype(jnp.float32)
        total = jnp.zeros((points, points), jnp.float32)
        for partner, mirror, start in ((low, to_low, 0), (high, to_high, points)):
            potential = matmul(back, backward[:, start : start + points]) * factor
            mirror[member] = packed(potential * mine).astype(jnp.bfloat16)
            total = total + potential * unpacked(partner[member].astype(jnp.float32))
        own[member] = -mixing * total


def combine_kernel(flags, own_a, own_b, a_low, a_high, b_low, b_high, out):
    for target, own in enumerate((own_a, own_b)):
        got = 0.0
        for n, (from_a, from_b) in enumerate(((a_low, b_low), (a_high, b_high))):
            kept = flags[n] == 1 - target
            got = got + jnp.where(
                kept, from_a[0].astype(jnp.float32), from_b[0].astype(jnp.float32)
            )
        out[target, 0] = own[0] - mixing * unpacked(got)


def whole_spec(array):
    rank = len(array.shape)
    return pl.BlockSpec(array.shape, lambda s: (0,) * rank)


def planes_spec(points, count=2):
    return pl.BlockSpec((count, points, points), lambda s: (s, 0, 0))


def packed_spec(points, count=2):
    return pl.BlockSpec((count, points * 3 // 2, 128), lambda s: (s, 0, 0))


def band_spec(band, points):
    return pl.BlockSpec((1, 2, points, points), lambda s: (band, s, 0, 0))


params = pltpu.CompilerParams(vmem_limit_bytes=48 * 1024 * 1024)


def per_device(bands, plan):
    slab_cells = bands.shape[1]
    points = bands.shape[2]
    band_count = lax.axis_size("band")
    my_block = lax.axis_index("band")
    forward, backward, plain, single, gather, scatter = [
        jnp.asarray(table) for table in device_tables(points, slab_cells)
    ]
    steps = slab_cells // 2
    devices = points // slab_cells
    packed_shape = jax.ShapeDtypeStruct((slab_cells, points * 3 // 2, 128), jnp.bfloat16)
    factor = host_factor(points)
    frequency = folded(jnp.arange(points, dtype=jnp.int32), points)
    column_ids = lax.axis_index("grid") * slab_cells + jnp.arange(slab_cells, dtype=jnp.int32)
    kernel_part = kernel_values(
        folded(column_ids, points)[:, None, None],
        frequency[None, :, None],
        jnp.concatenate([frequency, frequency[points // 128 * 128 :]])[None, None, :],
    )

    def swap(values, mask):
        return lax.ppermute(values, "band", [(i, i ^ mask) for i in range(band_count)])

    low = jnp.minimum(plan[0, 0], plan[1, 0])
    high = jnp.maximum(plan[0, 0], plan[1, 0])
    chip_low, chip_high = low // 2, high // 2
    chip_masks = range(1, band_count // 2)
    one_chip = chip_low == chip_high
    lone = jnp.logical_or(chip_low == 0, one_chip)
    pairs = [(i, j) for i in chip_masks for j in chip_masks if i < j]
    pair_index = sum(
        jnp.where(jnp.logical_and(chip_low == i, chip_high == j), n + len(chip_masks), 0)
        for n, (i, j) in enumerate(pairs)
    )
    branch_index = jnp.where(lone, chip_high - 1, pair_index)
    fetch_index = jnp.where(one_chip, chip_high - 1 + len(chip_masks) + len(pairs), branch_index)
    is_high = [my_block > jnp.bitwise_xor(my_block, mask) for mask in (low, high)]
    crossed = [mask % 2 == 1 for mask in (low, high)]

    def exchange_branches():
        singles = [lambda u, v, m=m: (u, swap(v, 2 * m)) for m in chip_masks]
        doubles = [lambda u, v, m=m: (swap(u, 2 * m[0]), swap(v, 2 * m[1])) for m in pairs]
        return singles + doubles

    def same_chip(mask):
        def branch(u, v):
            got = swap(v, 2 * mask)
            return swap(got, 1), got

        return branch

    sibling = swap(bands, 1)

    def fetch(values, other, band):
        picks = []
        for mask, flag in zip((low, high), is_high):
            picks.append(jnp.where(jnp.logical_xor(flag, mask == 1), band, 1 - band))
        flags = jnp.stack(picks + [flag.astype(jnp.int32) for flag in crossed])
        blocks = [
            pl.BlockSpec((1, 2, points, points), lambda s, f, n=n: (f[n], s, 0, 0))
            for n in (0, 0, 1, 1)
        ]
        sent = pl.pallas_call(
            pack_kernel,
            grid_spec=pltpu.PrefetchScalarGridSpec(
                num_scalar_prefetch=1,
                grid=(steps,),
                in_specs=blocks,
                out_specs=[pl.BlockSpec((2, points * 3 // 2, 128), lambda s, f: (s, 0, 0))] * 2,
            ),
            out_shape=[packed_shape] * 2,
            compiler_params=params,
        )(flags, values, other, values, other)
        branches = exchange_branches() + [same_chip(m) for m in chip_masks]
        return lax.switch(fetch_index, branches, *sent)

    def give_back(mirrors):
        sent = [jnp.where(c, swap(m, 1), m) for c, m in zip(crossed, mirrors)]
        total = (sent[0].astype(jnp.float32) + sent[1].astype(jnp.float32)).astype(jnp.bfloat16)
        first = jnp.where(one_chip, jnp.zeros_like(total), sent[0])
        second = jnp.where(one_chip, total, sent[1])
        return lax.switch(branch_index, exchange_branches(), first, second)

    def transform_in(band, partners):
        return pl.pallas_call(
            forward_kernel,
            grid=(steps,),
            in_specs=[
                band_spec(band, points),
                packed_spec(points),
                packed_spec(points),
                whole_spec(forward),
                whole_spec(plain),
            ],
            out_specs=pl.BlockSpec((points // 2, 2, 2, 2 * points), lambda s: (0, s, 0, 0)),
            out_shape=jax.ShapeDtypeStruct(
                (points // 2, slab_cells, 2, 2 * points), jnp.bfloat16
            ),
            compiler_params=params,
        )(bands, *partners, forward, plain)

    def send(values):
        return lax.all_to_all(values, "grid", split_axis=0, concat_axis=0, tiled=True)

    def screen_lines(received):
        block = (devices, 1, slab_cells, 2, 2 * points)
        return pl.pallas_call(
            screen_kernel,
            grid=(steps,),
            in_specs=[
                pl.BlockSpec(block, lambda s: (0, s, 0, 0, 0)),
                pl.BlockSpec((2,) + kernel_part.shape[1:], lambda s: (s, 0, 0)),
                whole_spec(gather),
                whole_spec(scatter),
            ],
            out_specs=pl.BlockSpec((points, 1, 2, 2 * points), lambda s: (0, s, 0, 0)),
            out_shape=jax.ShapeDtypeStruct((points, steps, 2, 2 * points), jnp.bfloat16),
            compiler_params=params,
        )(
            received.reshape(devices, steps, slab_cells, 2, 2 * points),
            kernel_part,
            gather,
            scatter,
        )

    def finish(band, partners, received):
        block = (devices, 2, steps, 2, 2 * points)
        return pl.pallas_call(
            lambda *refs: backward_kernel(factor, *refs),
            grid=(steps,),
            in_specs=[
                pl.BlockSpec(block, lambda s: (0, s, 0, 0, 0)),
                band_spec(band, points),
                packed_spec(points),
                packed_spec(points),
                whole_spec(single),
                whole_spec(backward),
            ],
            out_specs=[planes_spec(points)] + [packed_spec(points)] * 2,
            out_shape=[
                jax.ShapeDtypeStruct((slab_cells, points, points), jnp.float32),
                packed_shape,
                packed_shape,
            ],
            compiler_params=params,
        )(
            received.reshape(devices, slab_cells, steps, 2, 2 * points),
            bands,
            *partners,
            single,
            backward,
        )

    def combine(own_a, own_b, got_a, got_b):
        flags = jnp.stack(is_high).astype(jnp.int32)
        return pl.pallas_call(
            combine_kernel,
            grid=(slab_cells,),
            in_specs=[pl.BlockSpec(memory_space=pltpu.SMEM)]
            + [planes_spec(points, 1)] * 2
            + [packed_spec(points, 1)] * 4,
            out_specs=pl.BlockSpec((2, 1, points, points), lambda s: (0, s, 0, 0)),
            out_shape=jax.ShapeDtypeStruct(bands.shape, jnp.float32),
            compiler_params=params,
        )(flags, own_a, own_b, *got_a, *got_b)

    together = lax.optimization_barrier
    partners_a = fetch(bands, sibling, 0)
    planes_a, bands_b, sibling_b = together((transform_in(0, partners_a), bands, sibling))
    lines_a = send(planes_a)
    partners_b = fetch(bands_b, sibling_b, 1)
    lines_a, planes_b = together((lines_a, transform_in(1, partners_b)))
    lines_b = send(planes_b)
    lines_b, screened_a = together((lines_b, screen_lines(lines_a)))
    back_a = send(screened_a)
    back_a, screened_b = together((back_a, screen_lines(lines_b)))
    back_b = send(screened_b)
    own_a, *mirrors_a = finish(0, partners_a, back_a)
    got_a = give_back(mirrors_a)
    back_b, own_a, got_a = together((back_b, own_a, got_a))
    own_b, *mirrors_b = finish(1, partners_b, back_b)
    got_b = give_back(mirrors_b)
    return combine(own_a, own_b, got_a, got_b)


def solution(mesh):
    in_specs = (P("band", "grid", None, None), P())
    out_specs = P("band", "grid", None, None)
    return jax.shard_map(
        per_device, mesh=mesh, in_specs=in_specs, out_specs=out_specs, check_vma=False
    )
```

```python
import math

import jax
import jax.numpy as jnp
import numpy as np
from jax import lax
from jax.experimental import pallas as pl
from jax.experimental.pallas import tpu as pltpu
from jax.sharding import PartitionSpec as P

screening = 0.11
cell_edge = 46.9
mixing = 0.25
decay = (2.0 * math.pi / cell_edge) ** 2 / (4.0 * screening**2)


def folded(index_values, points):
    return jnp.where(index_values < points // 2, index_values, index_values - points)


def kernel_values(freq_x, freq_y, freq_z):
    squares = freq_x * freq_x + freq_y * freq_y + freq_z * freq_z
    scaled = squares.astype(jnp.float32) * jnp.float32(decay)
    safe_value = jnp.where(squares == 0, jnp.float32(1.0), scaled)
    return jnp.where(squares == 0, jnp.float32(1.0), (1.0 - jnp.exp(-safe_value)) / safe_value)


def host_factor(points):
    index_values = np.arange(points)
    freq = np.where(index_values < points // 2, index_values, index_values - points)
    sq = freq * freq
    squares = sq[:, None, None] + sq[None, :, None] + sq[None, None, :]
    values, counts = np.unique(squares, return_counts=True)
    scaled = np.where(values == 0, 1.0, values * decay)
    kernel = np.where(values == 0, 1.0, -np.expm1(-scaled) / scaled)
    power = float(np.sum(kernel * kernel * counts))
    return 1.0 / math.sqrt(power / points**3) / points**3


def host_tables(points):
    index_values = np.arange(points)
    product = index_values[:, None] * index_values[None, :] % points
    angles = product.astype(np.float64) * (2.0 * math.pi / points)
    return np.cos(angles).astype(jnp.bfloat16), np.sin(angles).astype(jnp.bfloat16)


def lane_order(points):
    whole = points // 128 * 128
    real, imag = np.arange(points), points + np.arange(points)
    return np.concatenate([real[:whole], imag[:whole], real[whole:], imag[whole:]])


def device_tables(points, slab):
    cos_np, sin_np = host_tables(points)
    order = lane_order(points)
    forward = np.concatenate(
        [np.concatenate([cos_np, -sin_np], 1), np.concatenate([sin_np, cos_np], 1)], 0
    )[:, order]
    backward = np.concatenate(
        [np.concatenate([cos_np, sin_np], 1), np.concatenate([-sin_np, cos_np], 1)], 0
    )[order]
    lines = np.arange(points).reshape(points // slab, slab // 2, 2).transpose(1, 0, 2).reshape(-1)
    single = [t[:, lines] for t in (cos_np, sin_np)]
    eye = np.eye(2, dtype=cos_np.dtype)
    slabs = np.arange(points).reshape(points // slab, slab).transpose(1, 0).reshape(-1)
    gather = [
        (t[:, slabs][None, :, :, None] * eye[:, None, None, :]).reshape(2 * points, 2 * points)
        for t in (cos_np, sin_np)
    ]
    scatter = [
        (t[:, None, None, :] * eye[None, :, :, None]).reshape(2 * points, 2 * points)
        for t in (cos_np, sin_np)
    ]
    plain = [cos_np, sin_np]
    return [forward, backward] + [np.stack(t) for t in (plain, single, gather, scatter)]


def matmul(left, right):
    return jnp.dot(left, right, preferred_element_type=jnp.float32)


def spin(tables, values, direction):
    with_cos = matmul(tables[0], values)
    with_sin = matmul(tables[1], values)
    whole = values.shape[1] // 256 * 128
    rest = values.shape[1] - 2 * whole
    real = with_cos[:, :whole] + direction * with_sin[:, whole : 2 * whole]
    imag = with_cos[:, whole : 2 * whole] - direction * with_sin[:, :whole]
    turned = pltpu.roll(with_sin[:, 2 * whole :], rest // 2, 1)
    lanes = lax.broadcasted_iota(jnp.int32, turned.shape, 1)
    turned = jnp.where(lanes < rest // 2, direction * turned, -direction * turned)
    return real, imag, with_cos[:, 2 * whole :] + turned


def joined(parts):
    return jnp.concatenate([part.astype(jnp.bfloat16) for part in parts], axis=1)


def packed(plane):
    whole = plane.shape[1] // 128 * 128
    half = plane.shape[0] // 2
    rest = jnp.concatenate([plane[:half, whole:], plane[half:, whole:]], axis=1)
    return jnp.concatenate([plane[:, :whole], rest], axis=0)


def unpacked(plane):
    rows = plane.shape[0] * 2 // 3
    half = plane.shape[1] // 2
    rest = jnp.concatenate([plane[rows:, :half], plane[rows:, half:]], axis=0)
    return jnp.concatenate([plane[:rows], rest], axis=1)


def pack_kernel(flags, own_low, other_low, own_high, other_high, low, high):
    for n, (own, other, out) in enumerate(
        ((own_low, other_low, low), (own_high, other_high, high))
    ):
        for member in range(out.shape[0]):
            mine = own[0, member].astype(jnp.float32)
            theirs = other[0, member].astype(jnp.float32)
            plane = jnp.where(flags[2 + n] == 1, theirs, mine)
            out[member] = packed(plane).astype(jnp.bfloat16)


def forward_kernel(own, low, high, forward, plain, out):
    points = own.shape[-1]
    for member in range(own.shape[1]):
        mine = own[0, member].astype(jnp.float32)

        def density(partner):
            return (mine * unpacked(partner[member].astype(jnp.float32))).astype(jnp.bfloat16)

        first = matmul(density(low), forward[:points]) + matmul(density(high), forward[points:])
        spectrum = joined(spin(plain, first.astype(jnp.bfloat16), 1.0))
        out[:, member] = spectrum.reshape(points // 2, 2, 2 * points)


def screen_kernel(lines, kernel, gather, scatter, out):
    points = out.shape[0]
    whole = points // 128 * 128
    gathered = jnp.concatenate(
        [lines[:, 0, plane].reshape(-1, 2 * points) for plane in range(lines.shape[2])], 0
    )
    real, imag, rest = spin(gather, gathered, 1.0)
    near = kernel[:, :, :whole].reshape(2 * points, whole)
    far = kernel[:, :, whole:].reshape(2 * points, whole)
    screened = joined([real * near, imag * near, rest * far])
    back = joined(spin(scatter, screened, -1.0))
    out[:, 0] = back.reshape(points, 2, 2 * points)


def backward_kernel(factor, lines, band, low, high, single, backward, own, to_low, to_high):
    points = band.shape[-1]
    for member in range(2):
        gathered = jnp.concatenate(
            [lines[:, member, pair].reshape(-1, 2 * points) for pair in range(lines.shape[2])], 0
        )
        back = joined(spin(single, gathered, -1.0))
        mine = band[0, member].astype(jnp.float32)
        total = jnp.zeros((points, points), jnp.float32)
        for partner, mirror, start in ((low, to_low, 0), (high, to_high, points)):
            potential = matmul(back, backward[:, start : start + points]) * factor
            mirror[member] = packed(potential * mine).astype(jnp.bfloat16)
            total = total + potential * unpacked(partner[member].astype(jnp.float32))
        own[member] = -mixing * total


def combine_kernel(flags, own_a, own_b, a_low, a_high, b_low, b_high, out):
    for member in range(own_a.shape[0]):
        for target, own in enumerate((own_a, own_b)):
            got = 0.0
            for n, (from_a, from_b) in enumerate(((a_low, b_low), (a_high, b_high))):
                kept = flags[n] == 1 - target
                mine, theirs = from_a[member], from_b[member]
                got = got + jnp.where(kept, mine.astype(jnp.float32), theirs.astype(jnp.float32))
            out[target, member] = own[member] - mixing * unpacked(got)


def whole_spec(array):
    rank = len(array.shape)
    return pl.BlockSpec(array.shape, lambda s: (0,) * rank)


def planes_spec(points, count=2):
    return pl.BlockSpec((count, points, points), lambda s: (s, 0, 0))


def packed_spec(points, count=2):
    return pl.BlockSpec((count, points * 3 // 2, 128), lambda s: (s, 0, 0))


def band_spec(band, points):
    return pl.BlockSpec((1, 2, points, points), lambda s: (band, s, 0, 0))


params = pltpu.CompilerParams(vmem_limit_bytes=60 * 1024 * 1024)


def per_device(bands, plan):
    slab_cells = bands.shape[1]
    points = bands.shape[2]
    band_count = lax.axis_size("band")
    my_block = lax.axis_index("band")
    forward, backward, plain, single, gather, scatter = [
        jnp.asarray(table) for table in device_tables(points, slab_cells)
    ]
    steps = slab_cells // 2
    devices = points // slab_cells
    packed_shape = jax.ShapeDtypeStruct((slab_cells, points * 3 // 2, 128), jnp.bfloat16)
    factor = host_factor(points)
    frequency = folded(jnp.arange(points, dtype=jnp.int32), points)
    column_ids = lax.axis_index("grid") * slab_cells + jnp.arange(slab_cells, dtype=jnp.int32)
    kernel_part = kernel_values(
        folded(column_ids, points)[:, None, None],
        frequency[None, :, None],
        jnp.concatenate([frequency, frequency[points // 128 * 128 :]])[None, None, :],
    )

    def swap(values, mask):
        return lax.ppermute(values, "band", [(i, i ^ mask) for i in range(band_count)])

    low = jnp.minimum(plan[0, 0], plan[1, 0])
    high = jnp.maximum(plan[0, 0], plan[1, 0])
    chip_low, chip_high = low // 2, high // 2
    chip_masks = range(1, band_count // 2)
    one_chip = chip_low == chip_high
    lone = jnp.logical_or(chip_low == 0, one_chip)
    pairs = [(i, j) for i in chip_masks for j in chip_masks if i < j]
    pair_index = sum(
        jnp.where(jnp.logical_and(chip_low == i, chip_high == j), n + len(chip_masks), 0)
        for n, (i, j) in enumerate(pairs)
    )
    branch_index = jnp.where(lone, chip_high - 1, pair_index)
    fetch_index = jnp.where(one_chip, chip_high - 1 + len(chip_masks) + len(pairs), branch_index)
    is_high = [my_block > jnp.bitwise_xor(my_block, mask) for mask in (low, high)]
    crossed = [mask % 2 == 1 for mask in (low, high)]

    def exchange_branches():
        singles = [lambda u, v, m=m: (u, swap(v, 2 * m)) for m in chip_masks]
        doubles = [lambda u, v, m=m: (swap(u, 2 * m[0]), swap(v, 2 * m[1])) for m in pairs]
        return singles + doubles

    def same_chip(mask):
        def branch(u, v):
            got = swap(v, 2 * mask)
            return swap(got, 1), got

        return branch

    sibling = swap(bands, 1)

    def fetch(values, other, band):
        picks = []
        for mask, flag in zip((low, high), is_high):
            picks.append(jnp.where(jnp.logical_xor(flag, mask == 1), band, 1 - band))
        flags = jnp.stack(picks + [flag.astype(jnp.int32) for flag in crossed])
        blocks = [
            pl.BlockSpec((1, 2, points, points), lambda s, f, n=n: (f[n], s, 0, 0))
            for n in (0, 0, 1, 1)
        ]
        sent = pl.pallas_call(
            pack_kernel,
            grid_spec=pltpu.PrefetchScalarGridSpec(
                num_scalar_prefetch=1,
                grid=(steps,),
                in_specs=blocks,
                out_specs=[pl.BlockSpec((2, points * 3 // 2, 128), lambda s, f: (s, 0, 0))] * 2,
            ),
            out_shape=[packed_shape] * 2,
            compiler_params=params,
        )(flags, values, other, values, other)
        branches = exchange_branches() + [same_chip(m) for m in chip_masks]
        return lax.switch(fetch_index, branches, *sent)

    def give_back(mirrors):
        sent = [jnp.where(c, swap(m, 1), m) for c, m in zip(crossed, mirrors)]
        total = (sent[0].astype(jnp.float32) + sent[1].astype(jnp.float32)).astype(jnp.bfloat16)
        first = jnp.where(one_chip, jnp.zeros_like(total), sent[0])
        second = jnp.where(one_chip, total, sent[1])
        return lax.switch(branch_index, exchange_branches(), first, second)

    def transform_in(band, partners):
        return pl.pallas_call(
            forward_kernel,
            grid=(steps,),
            in_specs=[
                band_spec(band, points),
                packed_spec(points),
                packed_spec(points),
                whole_spec(forward),
                whole_spec(plain),
            ],
            out_specs=pl.BlockSpec((points // 2, 2, 2, 2 * points), lambda s: (0, s, 0, 0)),
            out_shape=jax.ShapeDtypeStruct(
                (points // 2, slab_cells, 2, 2 * points), jnp.bfloat16
            ),
            compiler_params=params,
        )(bands, *partners, forward, plain)

    def send(values):
        return lax.all_to_all(values, "grid", split_axis=0, concat_axis=0, tiled=True)

    def screen_lines(received):
        block = (devices, 1, slab_cells, 2, 2 * points)
        return pl.pallas_call(
            screen_kernel,
            grid=(steps,),
            in_specs=[
                pl.BlockSpec(block, lambda s: (0, s, 0, 0, 0)),
                pl.BlockSpec((2,) + kernel_part.shape[1:], lambda s: (s, 0, 0)),
                whole_spec(gather),
                whole_spec(scatter),
            ],
            out_specs=pl.BlockSpec((points, 1, 2, 2 * points), lambda s: (0, s, 0, 0)),
            out_shape=jax.ShapeDtypeStruct((points, steps, 2, 2 * points), jnp.bfloat16),
            compiler_params=params,
        )(
            received.reshape(devices, steps, slab_cells, 2, 2 * points),
            kernel_part,
            gather,
            scatter,
        )

    def finish(band, partners, received):
        block = (devices, 2, steps, 2, 2 * points)
        return pl.pallas_call(
            lambda *refs: backward_kernel(factor, *refs),
            grid=(steps,),
            in_specs=[
                pl.BlockSpec(block, lambda s: (0, s, 0, 0, 0)),
                band_spec(band, points),
                packed_spec(points),
                packed_spec(points),
                whole_spec(single),
                whole_spec(backward),
            ],
            out_specs=[planes_spec(points)] + [packed_spec(points)] * 2,
            out_shape=[
                jax.ShapeDtypeStruct((slab_cells, points, points), jnp.float32),
                packed_shape,
                packed_shape,
            ],
            compiler_params=params,
        )(
            received.reshape(devices, slab_cells, steps, 2, 2 * points),
            bands,
            *partners,
            single,
            backward,
        )

    def combine(own_a, own_b, got_a, got_b):
        flags = jnp.stack(is_high).astype(jnp.int32)
        return pl.pallas_call(
            combine_kernel,
            grid=(steps,),
            in_specs=[pl.BlockSpec(memory_space=pltpu.SMEM)]
            + [planes_spec(points)] * 2
            + [packed_spec(points)] * 4,
            out_specs=pl.BlockSpec((2, 2, points, points), lambda s: (0, s, 0, 0)),
            out_shape=jax.ShapeDtypeStruct(bands.shape, jnp.float32),
            compiler_params=params,
        )(flags, own_a, own_b, *got_a, *got_b)

    together = lax.optimization_barrier
    partners_a = fetch(bands, sibling, 0)
    planes_a, bands_b, sibling_b = together((transform_in(0, partners_a), bands, sibling))
    lines_a = send(planes_a)
    partners_b = fetch(bands_b, sibling_b, 1)
    lines_a, planes_b = together((lines_a, transform_in(1, partners_b)))
    lines_b = send(planes_b)
    lines_b, screened_a = together((lines_b, screen_lines(lines_a)))
    back_a = send(screened_a)
    back_a, screened_b = together((back_a, screen_lines(lines_b)))
    back_b = send(screened_b)
    own_a, *mirrors_a = finish(0, partners_a, back_a)
    got_a = give_back(mirrors_a)
    back_b, own_a, got_a = together((back_b, own_a, got_a))
    own_b, *mirrors_b = finish(1, partners_b, back_b)
    got_b = give_back(mirrors_b)
    return combine(own_a, own_b, got_a, got_b)


def solution(mesh):
    in_specs = (P("band", "grid", None, None), P())
    out_specs = P("band", "grid", None, None)
    return jax.shard_map(
        per_device, mesh=mesh, in_specs=in_specs, out_specs=out_specs, check_vma=False
    )
```

```python
import math

import jax
import jax.numpy as jnp
import numpy as np
from jax import lax
from jax.experimental import pallas as pl
from jax.experimental.pallas import tpu as pltpu
from jax.sharding import PartitionSpec as P

screening = 0.11
cell_edge = 46.9
mixing = 0.25
decay = (2.0 * math.pi / cell_edge) ** 2 / (4.0 * screening**2)


def folded(index_values, points):
    return jnp.where(index_values < points // 2, index_values, index_values - points)


def kernel_values(freq_x, freq_y, freq_z):
    squares = freq_x * freq_x + freq_y * freq_y + freq_z * freq_z
    scaled = squares.astype(jnp.float32) * jnp.float32(decay)
    safe_value = jnp.where(squares == 0, jnp.float32(1.0), scaled)
    return jnp.where(squares == 0, jnp.float32(1.0), (1.0 - jnp.exp(-safe_value)) / safe_value)


def host_factor(points):
    index_values = np.arange(points)
    freq = np.where(index_values < points // 2, index_values, index_values - points)
    sq = freq * freq
    squares = sq[:, None, None] + sq[None, :, None] + sq[None, None, :]
    values, counts = np.unique(squares, return_counts=True)
    scaled = np.where(values == 0, 1.0, values * decay)
    kernel = np.where(values == 0, 1.0, -np.expm1(-scaled) / scaled)
    power = float(np.sum(kernel * kernel * counts))
    return 1.0 / math.sqrt(power / points**3) / points**3


def host_tables(points):
    index_values = np.arange(points)
    product = index_values[:, None] * index_values[None, :] % points
    angles = product.astype(np.float64) * (2.0 * math.pi / points)
    return np.cos(angles).astype(jnp.bfloat16), np.sin(angles).astype(jnp.bfloat16)


def lane_order(points):
    whole = points // 128 * 128
    real, imag = np.arange(points), points + np.arange(points)
    return np.concatenate([real[:whole], imag[:whole], real[whole:], imag[whole:]])


def device_tables(points, slab):
    cos_np, sin_np = host_tables(points)
    order = lane_order(points)
    forward = np.concatenate(
        [np.concatenate([cos_np, -sin_np], 1), np.concatenate([sin_np, cos_np], 1)], 0
    )[:, order]
    backward = np.concatenate(
        [np.concatenate([cos_np, sin_np], 1), np.concatenate([-sin_np, cos_np], 1)], 0
    )[order]
    lines = np.arange(points).reshape(points // slab, slab // 2, 2).transpose(1, 0, 2).reshape(-1)
    single = [t[:, lines] for t in (cos_np, sin_np)]
    eye = np.eye(2, dtype=cos_np.dtype)
    slabs = np.arange(points).reshape(points // slab, slab).transpose(1, 0).reshape(-1)
    gather = [
        (t[:, slabs][None, :, :, None] * eye[:, None, None, :]).reshape(2 * points, 2 * points)
        for t in (cos_np, sin_np)
    ]
    scatter = [
        (t[:, None, None, :] * eye[None, :, :, None]).reshape(2 * points, 2 * points)
        for t in (cos_np, sin_np)
    ]
    plain = [cos_np, sin_np]
    return [forward, backward] + [np.stack(t) for t in (plain, single, gather, scatter)]


def matmul(left, right):
    return jnp.dot(left, right, preferred_element_type=jnp.float32)


def spin(tables, values, direction):
    with_cos = matmul(tables[0], values)
    with_sin = matmul(tables[1], values)
    whole = values.shape[1] // 256 * 128
    rest = values.shape[1] - 2 * whole
    real = with_cos[:, :whole] + direction * with_sin[:, whole : 2 * whole]
    imag = with_cos[:, whole : 2 * whole] - direction * with_sin[:, :whole]
    turned = pltpu.roll(with_sin[:, 2 * whole :], rest // 2, 1)
    lanes = lax.broadcasted_iota(jnp.int32, turned.shape, 1)
    turned = jnp.where(lanes < rest // 2, direction * turned, -direction * turned)
    return real, imag, with_cos[:, 2 * whole :] + turned


def joined(parts):
    return jnp.concatenate([part.astype(jnp.bfloat16) for part in parts], axis=1)


def packed(plane):
    whole = plane.shape[1] // 128 * 128
    half = plane.shape[0] // 2
    rest = jnp.concatenate([plane[:half, whole:], plane[half:, whole:]], axis=1)
    return jnp.concatenate([plane[:, :whole], rest], axis=0)


def unpacked(plane):
    rows = plane.shape[0] * 2 // 3
    half = plane.shape[1] // 2
    rest = jnp.concatenate([plane[rows:, :half], plane[rows:, half:]], axis=0)
    return jnp.concatenate([plane[:rows], rest], axis=1)


def pack_kernel(flags, own_low, other_low, own_high, other_high, low, high):
    for n, (own, other, out) in enumerate(
        ((own_low, other_low, low), (own_high, other_high, high))
    ):
        for member in range(out.shape[0]):
            mine = own[0, member].astype(jnp.float32)
            theirs = other[0, member].astype(jnp.float32)
            plane = jnp.where(flags[2 + n] == 1, theirs, mine)
            out[member] = packed(plane).astype(jnp.bfloat16)


def forward_kernel(own, low, high, forward, plain, out):
    points = own.shape[-1]
    for member in range(own.shape[1]):
        mine = own[0, member].astype(jnp.float32)

        def density(partner):
            return (mine * unpacked(partner[member].astype(jnp.float32))).astype(jnp.bfloat16)

        first = matmul(density(low), forward[:points]) + matmul(density(high), forward[points:])
        spectrum = joined(spin(plain, first.astype(jnp.bfloat16), 1.0))
        out[:, member] = spectrum.reshape(points // 2, 2, 2 * points)


def screen_kernel(lines, kernel, gather, scatter, out):
    points = out.shape[0]
    whole = points // 128 * 128
    gathered = jnp.concatenate(
        [lines[:, 0, plane].reshape(-1, 2 * points) for plane in range(lines.shape[2])], 0
    )
    real, imag, rest = spin(gather, gathered, 1.0)
    near = kernel[:, :, :whole].reshape(2 * points, whole)
    far = kernel[:, :, whole:].reshape(2 * points, whole)
    screened = joined([real * near, imag * near, rest * far])
    back = joined(spin(scatter, screened, -1.0))
    out[:, 0] = back.reshape(points, 2, 2 * points)


def backward_kernel(factor, lines, band, low, high, single, backward, own, to_low, to_high):
    points = band.shape[-1]
    for member in range(2):
        gathered = jnp.concatenate(
            [lines[:, member, pair].reshape(-1, 2 * points) for pair in range(lines.shape[2])], 0
        )
        back = joined(spin(single, gathered, -1.0))
        mine = band[0, member].astype(jnp.float32)
        total = jnp.zeros((points, points), jnp.float32)
        for partner, mirror, start in ((low, to_low, 0), (high, to_high, points)):
            potential = matmul(back, backward[:, start : start + points]) * factor
            mirror[member] = packed(potential * mine).astype(jnp.bfloat16)
            total = total + potential * unpacked(partner[member].astype(jnp.float32))
        own[member] = -mixing * total


def combine_kernel(flags, own_a, own_b, a_low, a_high, b_low, b_high, out):
    for member in range(own_a.shape[0]):
        for target, own in enumerate((own_a, own_b)):
            got = 0.0
            for n, (from_a, from_b) in enumerate(((a_low, b_low), (a_high, b_high))):
                kept = flags[n] == 1 - target
                mine, theirs = from_a[member], from_b[member]
                got = got + jnp.where(kept, mine.astype(jnp.float32), theirs.astype(jnp.float32))
            out[target, member] = own[member] - mixing * unpacked(got)


def whole_spec(array):
    rank = len(array.shape)
    return pl.BlockSpec(array.shape, lambda s: (0,) * rank)


def planes_spec(points, count=2):
    return pl.BlockSpec((count, points, points), lambda s: (s, 0, 0))


def packed_spec(points, count=2):
    return pl.BlockSpec((count, points * 3 // 2, 128), lambda s: (s, 0, 0))


def band_spec(band, points):
    return pl.BlockSpec((1, 2, points, points), lambda s: (band, s, 0, 0))


params = pltpu.CompilerParams(vmem_limit_bytes=32 * 1024 * 1024)


def per_device(bands, plan):
    slab_cells = bands.shape[1]
    points = bands.shape[2]
    band_count = lax.axis_size("band")
    my_block = lax.axis_index("band")
    forward, backward, plain, single, gather, scatter = [
        jnp.asarray(table) for table in device_tables(points, slab_cells)
    ]
    steps = slab_cells // 2
    devices = points // slab_cells
    packed_shape = jax.ShapeDtypeStruct((slab_cells, points * 3 // 2, 128), jnp.bfloat16)
    factor = host_factor(points)
    frequency = folded(jnp.arange(points, dtype=jnp.int32), points)
    column_ids = lax.axis_index("grid") * slab_cells + jnp.arange(slab_cells, dtype=jnp.int32)
    kernel_part = kernel_values(
        folded(column_ids, points)[:, None, None],
        frequency[None, :, None],
        jnp.concatenate([frequency, frequency[points // 128 * 128 :]])[None, None, :],
    )

    def swap(values, mask):
        return lax.ppermute(values, "band", [(i, i ^ mask) for i in range(band_count)])

    low = jnp.minimum(plan[0, 0], plan[1, 0])
    high = jnp.maximum(plan[0, 0], plan[1, 0])
    chip_low, chip_high = low // 2, high // 2
    chip_masks = range(1, band_count // 2)
    one_chip = chip_low == chip_high
    lone = jnp.logical_or(chip_low == 0, one_chip)
    pairs = [(i, j) for i in chip_masks for j in chip_masks if i < j]
    pair_index = sum(
        jnp.where(jnp.logical_and(chip_low == i, chip_high == j), n + len(chip_masks), 0)
        for n, (i, j) in enumerate(pairs)
    )
    branch_index = jnp.where(lone, chip_high - 1, pair_index)
    fetch_index = jnp.where(one_chip, chip_high - 1 + len(chip_masks) + len(pairs), branch_index)
    is_high = [my_block > jnp.bitwise_xor(my_block, mask) for mask in (low, high)]
    crossed = [mask % 2 == 1 for mask in (low, high)]

    def exchange_branches():
        singles = [lambda u, v, m=m: (u, swap(v, 2 * m)) for m in chip_masks]
        doubles = [lambda u, v, m=m: (swap(u, 2 * m[0]), swap(v, 2 * m[1])) for m in pairs]
        return singles + doubles

    def same_chip(mask):
        def branch(u, v):
            got = swap(v, 2 * mask)
            return swap(got, 1), got

        return branch

    sibling = swap(bands, 1)

    def fetch(values, other, band):
        picks = []
        for mask, flag in zip((low, high), is_high):
            picks.append(jnp.where(jnp.logical_xor(flag, mask == 1), band, 1 - band))
        flags = jnp.stack(picks + [flag.astype(jnp.int32) for flag in crossed])
        blocks = [
            pl.BlockSpec((1, 2, points, points), lambda s, f, n=n: (f[n], s, 0, 0))
            for n in (0, 0, 1, 1)
        ]
        sent = pl.pallas_call(
            pack_kernel,
            grid_spec=pltpu.PrefetchScalarGridSpec(
                num_scalar_prefetch=1,
                grid=(steps,),
                in_specs=blocks,
                out_specs=[pl.BlockSpec((2, points * 3 // 2, 128), lambda s, f: (s, 0, 0))] * 2,
            ),
            out_shape=[packed_shape] * 2,
            compiler_params=params,
        )(flags, values, other, values, other)
        branches = exchange_branches() + [same_chip(m) for m in chip_masks]
        return lax.switch(fetch_index, branches, *sent)

    def give_back(mirrors):
        sent = [jnp.where(c, swap(m, 1), m) for c, m in zip(crossed, mirrors)]
        total = (sent[0].astype(jnp.float32) + sent[1].astype(jnp.float32)).astype(jnp.bfloat16)
        first = jnp.where(one_chip, jnp.zeros_like(total), sent[0])
        second = jnp.where(one_chip, total, sent[1])
        return lax.switch(branch_index, exchange_branches(), first, second)

    def transform_in(band, partners):
        return pl.pallas_call(
            forward_kernel,
            grid=(steps,),
            in_specs=[
                band_spec(band, points),
                packed_spec(points),
                packed_spec(points),
                whole_spec(forward),
                whole_spec(plain),
            ],
            out_specs=pl.BlockSpec((points // 2, 2, 2, 2 * points), lambda s: (0, s, 0, 0)),
            out_shape=jax.ShapeDtypeStruct(
                (points // 2, slab_cells, 2, 2 * points), jnp.bfloat16
            ),
            compiler_params=params,
        )(bands, *partners, forward, plain)

    def send(values):
        return lax.all_to_all(values, "grid", split_axis=0, concat_axis=0, tiled=True)

    def screen_lines(received):
        block = (devices, 1, slab_cells, 2, 2 * points)
        return pl.pallas_call(
            screen_kernel,
            grid=(steps,),
            in_specs=[
                pl.BlockSpec(block, lambda s: (0, s, 0, 0, 0)),
                pl.BlockSpec((2,) + kernel_part.shape[1:], lambda s: (s, 0, 0)),
                whole_spec(gather),
                whole_spec(scatter),
            ],
            out_specs=pl.BlockSpec((points, 1, 2, 2 * points), lambda s: (0, s, 0, 0)),
            out_shape=jax.ShapeDtypeStruct((points, steps, 2, 2 * points), jnp.bfloat16),
            compiler_params=params,
        )(
            received.reshape(devices, steps, slab_cells, 2, 2 * points),
            kernel_part,
            gather,
            scatter,
        )

    def finish(band, partners, received):
        block = (devices, 2, steps, 2, 2 * points)
        return pl.pallas_call(
            lambda *refs: backward_kernel(factor, *refs),
            grid=(steps,),
            in_specs=[
                pl.BlockSpec(block, lambda s: (0, s, 0, 0, 0)),
                band_spec(band, points),
                packed_spec(points),
                packed_spec(points),
                whole_spec(single),
                whole_spec(backward),
            ],
            out_specs=[planes_spec(points)] + [packed_spec(points)] * 2,
            out_shape=[
                jax.ShapeDtypeStruct((slab_cells, points, points), jnp.float32),
                packed_shape,
                packed_shape,
            ],
            compiler_params=params,
        )(
            received.reshape(devices, slab_cells, steps, 2, 2 * points),
            bands,
            *partners,
            single,
            backward,
        )

    def combine(own_a, own_b, got_a, got_b):
        flags = jnp.stack(is_high).astype(jnp.int32)
        return pl.pallas_call(
            combine_kernel,
            grid=(steps,),
            in_specs=[pl.BlockSpec(memory_space=pltpu.SMEM)]
            + [planes_spec(points)] * 2
            + [packed_spec(points)] * 4,
            out_specs=pl.BlockSpec((2, 2, points, points), lambda s: (0, s, 0, 0)),
            out_shape=jax.ShapeDtypeStruct(bands.shape, jnp.float32),
            compiler_params=params,
        )(flags, own_a, own_b, *got_a, *got_b)

    together = lax.optimization_barrier
    partners_a = fetch(bands, sibling, 0)
    planes_a, bands_b, sibling_b = together((transform_in(0, partners_a), bands, sibling))
    lines_a = send(planes_a)
    partners_b = fetch(bands_b, sibling_b, 1)
    lines_a, planes_b = together((lines_a, transform_in(1, partners_b)))
    lines_b = send(planes_b)
    lines_b, screened_a = together((lines_b, screen_lines(lines_a)))
    back_a = send(screened_a)
    back_a, screened_b = together((back_a, screen_lines(lines_b)))
    back_b = send(screened_b)
    own_a, *mirrors_a = finish(0, partners_a, back_a)
    got_a = give_back(mirrors_a)
    back_b, own_a, got_a = together((back_b, own_a, got_a))
    own_b, *mirrors_b = finish(1, partners_b, back_b)
    got_b = give_back(mirrors_b)
    return combine(own_a, own_b, got_a, got_b)


def solution(mesh):
    in_specs = (P("band", "grid", None, None), P())
    out_specs = P("band", "grid", None, None)
    return jax.shard_map(
        per_device, mesh=mesh, in_specs=in_specs, out_specs=out_specs, check_vma=False
    )
```

```python
import math

import jax
import jax.numpy as jnp
import numpy as np
from jax import lax
from jax.experimental import pallas as pl
from jax.experimental.pallas import tpu as pltpu
from jax.sharding import PartitionSpec as P

screening = 0.11
cell_edge = 46.9
mixing = 0.25
decay = (2.0 * math.pi / cell_edge) ** 2 / (4.0 * screening**2)


def folded(index_values, points):
    return jnp.where(index_values < points // 2, index_values, index_values - points)


def kernel_values(freq_x, freq_y, freq_z):
    squares = freq_x * freq_x + freq_y * freq_y + freq_z * freq_z
    scaled = squares.astype(jnp.float32) * jnp.float32(decay)
    safe_value = jnp.where(squares == 0, jnp.float32(1.0), scaled)
    return jnp.where(squares == 0, jnp.float32(1.0), (1.0 - jnp.exp(-safe_value)) / safe_value)


def host_factor(points):
    index_values = np.arange(points)
    freq = np.where(index_values < points // 2, index_values, index_values - points)
    sq = freq * freq
    squares = sq[:, None, None] + sq[None, :, None] + sq[None, None, :]
    values, counts = np.unique(squares, return_counts=True)
    scaled = np.where(values == 0, 1.0, values * decay)
    kernel = np.where(values == 0, 1.0, -np.expm1(-scaled) / scaled)
    power = float(np.sum(kernel * kernel * counts))
    return 1.0 / math.sqrt(power / points**3) / points**3


def host_tables(points):
    index_values = np.arange(points)
    product = index_values[:, None] * index_values[None, :] % points
    angles = product.astype(np.float64) * (2.0 * math.pi / points)
    return np.cos(angles).astype(jnp.bfloat16), np.sin(angles).astype(jnp.bfloat16)


def lane_order(points):
    whole = points // 128 * 128
    real, imag = np.arange(points), points + np.arange(points)
    return np.concatenate([real[:whole], imag[:whole], real[whole:], imag[whole:]])


def device_tables(points, slab):
    cos_np, sin_np = host_tables(points)
    order = lane_order(points)
    forward = np.concatenate(
        [np.concatenate([cos_np, -sin_np], 1), np.concatenate([sin_np, cos_np], 1)], 0
    )[:, order]
    backward = np.concatenate(
        [np.concatenate([cos_np, sin_np], 1), np.concatenate([-sin_np, cos_np], 1)], 0
    )[order]
    lines = np.arange(points).reshape(points // slab, slab // 2, 2).transpose(1, 0, 2).reshape(-1)
    single = [t[:, lines] for t in (cos_np, sin_np)]
    eye = np.eye(2, dtype=cos_np.dtype)
    slabs = np.arange(points).reshape(points // slab, slab).transpose(1, 0).reshape(-1)
    gather = [
        (t[:, slabs][None, :, :, None] * eye[:, None, None, :]).reshape(2 * points, 2 * points)
        for t in (cos_np, sin_np)
    ]
    scatter = [
        (t[:, None, None, :] * eye[None, :, :, None]).reshape(2 * points, 2 * points)
        for t in (cos_np, sin_np)
    ]
    plain = [cos_np, sin_np]
    tables = [np.concatenate(t) for t in (plain, single, gather, scatter)]
    return [forward, backward] + tables


def matmul(left, right):
    return jnp.dot(left, right, preferred_element_type=jnp.float32)


def spin(tables, values, direction):
    rows = tables.shape[0] // 2
    both = matmul(tables[...], values)
    with_cos, with_sin = both[:rows], both[rows:]
    whole = values.shape[1] // 256 * 128
    rest = values.shape[1] - 2 * whole
    real = with_cos[:, :whole] + direction * with_sin[:, whole : 2 * whole]
    imag = with_cos[:, whole : 2 * whole] - direction * with_sin[:, :whole]
    turned = pltpu.roll(with_sin[:, 2 * whole :], rest // 2, 1)
    lanes = lax.broadcasted_iota(jnp.int32, turned.shape, 1)
    turned = jnp.where(lanes < rest // 2, direction * turned, -direction * turned)
    return real, imag, with_cos[:, 2 * whole :] + turned


def joined(parts):
    return jnp.concatenate([part.astype(jnp.bfloat16) for part in parts], axis=1)


def packed(plane):
    whole = plane.shape[1] // 128 * 128
    half = plane.shape[0] // 2
    rest = jnp.concatenate([plane[:half, whole:], plane[half:, whole:]], axis=1)
    return jnp.concatenate([plane[:, :whole], rest], axis=0)


def unpacked(plane):
    rows = plane.shape[0] * 2 // 3
    half = plane.shape[1] // 2
    rest = jnp.concatenate([plane[rows:, :half], plane[rows:, half:]], axis=0)
    return jnp.concatenate([plane[:rows], rest], axis=1)


def pack_kernel(flags, own_low, other_low, own_high, other_high, low, high):
    for n, (own, other, out) in enumerate(
        ((own_low, other_low, low), (own_high, other_high, high))
    ):
        for member in range(out.shape[0]):
            mine = own[0, member].astype(jnp.float32)
            theirs = other[0, member].astype(jnp.float32)
            plane = jnp.where(flags[2 + n] == 1, theirs, mine)
            out[member] = packed(plane).astype(jnp.bfloat16)


def forward_kernel(own, low, high, forward, plain, out):
    points = own.shape[-1]
    members = range(own.shape[1])

    def density(partner):
        planes = []
        for n in members:
            theirs = unpacked(partner[n].astype(jnp.float32))
            planes.append((own[0, n].astype(jnp.float32) * theirs).astype(jnp.bfloat16))
        return jnp.concatenate(planes, axis=0)

    first = matmul(density(low), forward[:points]) + matmul(density(high), forward[points:])
    first = first.astype(jnp.bfloat16)
    for n in members:
        spectrum = joined(spin(plain, first[n * points : (n + 1) * points], 1.0))
        out[:, n] = spectrum.reshape(points // 2, 2, 2 * points)


def screen_kernel(lines, kernel, gather, scatter, out):
    points = out.shape[0]
    whole = points // 128 * 128
    gathered = jnp.concatenate(
        [lines[:, 0, plane].reshape(-1, 2 * points) for plane in range(lines.shape[2])], 0
    )
    real, imag, rest = spin(gather, gathered, 1.0)
    near = kernel[:, :, :whole].reshape(2 * points, whole)
    far = kernel[:, :, whole:].reshape(2 * points, whole)
    screened = joined([real * near, imag * near, rest * far])
    back = joined(spin(scatter, screened, -1.0))
    out[:, 0] = back.reshape(points, 2, 2 * points)


def backward_kernel(factor, lines, band, low, high, single, backward, own, to_low, to_high):
    points = band.shape[-1]
    members = range(band.shape[1])
    backs = []
    for n in members:
        gathered = jnp.concatenate(
            [lines[:, n, pair].reshape(-1, 2 * points) for pair in range(lines.shape[2])], 0
        )
        backs.append(joined(spin(single, gathered, -1.0)))
    back = jnp.concatenate(backs, axis=0)
    potentials = [
        matmul(back, backward[:, start : start + points]) * factor for start in (0, points)
    ]
    for n in members:
        mine = band[0, n].astype(jnp.float32)
        total = jnp.zeros((points, points), jnp.float32)
        for potential, partner, mirror in zip(potentials, (low, high), (to_low, to_high)):
            here = potential[n * points : (n + 1) * points]
            mirror[n] = packed(here * mine).astype(jnp.bfloat16)
            total = total + here * unpacked(partner[n].astype(jnp.float32))
        own[n] = -mixing * total


def combine_kernel(flags, own_a, own_b, a_low, a_high, b_low, b_high, out):
    for member in range(own_a.shape[0]):
        for target, own in enumerate((own_a, own_b)):
            got = 0.0
            for n, (from_a, from_b) in enumerate(((a_low, b_low), (a_high, b_high))):
                kept = flags[n] == 1 - target
                mine, theirs = from_a[member], from_b[member]
                got = got + jnp.where(kept, mine.astype(jnp.float32), theirs.astype(jnp.float32))
            out[target, member] = own[member] - mixing * unpacked(got)


def whole_spec(array):
    rank = len(array.shape)
    return pl.BlockSpec(array.shape, lambda s: (0,) * rank)


def planes_spec(points, count=2):
    return pl.BlockSpec((count, points, points), lambda s: (s, 0, 0))


def packed_spec(points, count=2):
    return pl.BlockSpec((count, points * 3 // 2, 128), lambda s: (s, 0, 0))


def band_spec(band, points):
    return pl.BlockSpec((1, 2, points, points), lambda s: (band, s, 0, 0))


params = pltpu.CompilerParams(vmem_limit_bytes=32 * 1024 * 1024)


def per_device(bands, plan):
    slab_cells = bands.shape[1]
    points = bands.shape[2]
    band_count = lax.axis_size("band")
    my_block = lax.axis_index("band")
    forward, backward, plain, single, gather, scatter = [
        jnp.asarray(table) for table in device_tables(points, slab_cells)
    ]
    steps = slab_cells // 2
    devices = points // slab_cells
    packed_shape = jax.ShapeDtypeStruct((slab_cells, points * 3 // 2, 128), jnp.bfloat16)
    factor = host_factor(points)
    frequency = folded(jnp.arange(points, dtype=jnp.int32), points)
    column_ids = lax.axis_index("grid") * slab_cells + jnp.arange(slab_cells, dtype=jnp.int32)
    kernel_part = kernel_values(
        folded(column_ids, points)[:, None, None],
        frequency[None, :, None],
        jnp.concatenate([frequency, frequency[points // 128 * 128 :]])[None, None, :],
    )

    def swap(values, mask):
        return lax.ppermute(values, "band", [(i, i ^ mask) for i in range(band_count)])

    low = jnp.minimum(plan[0, 0], plan[1, 0])
    high = jnp.maximum(plan[0, 0], plan[1, 0])
    chip_low, chip_high = low // 2, high // 2
    chip_masks = range(1, band_count // 2)
    one_chip = chip_low == chip_high
    lone = jnp.logical_or(chip_low == 0, one_chip)
    pairs = [(i, j) for i in chip_masks for j in chip_masks if i < j]
    pair_index = sum(
        jnp.where(jnp.logical_and(chip_low == i, chip_high == j), n + len(chip_masks), 0)
        for n, (i, j) in enumerate(pairs)
    )
    branch_index = jnp.where(lone, chip_high - 1, pair_index)
    fetch_index = jnp.where(one_chip, chip_high - 1 + len(chip_masks) + len(pairs), branch_index)
    is_high = [my_block > jnp.bitwise_xor(my_block, mask) for mask in (low, high)]
    crossed = [mask % 2 == 1 for mask in (low, high)]

    def exchange_branches():
        singles = [lambda u, v, m=m: (u, swap(v, 2 * m)) for m in chip_masks]
        doubles = [lambda u, v, m=m: (swap(u, 2 * m[0]), swap(v, 2 * m[1])) for m in pairs]
        return singles + doubles

    def same_chip(mask):
        def branch(u, v):
            got = swap(v, 2 * mask)
            return swap(got, 1), got

        return branch

    sibling = swap(bands, 1)

    def fetch(values, other, band):
        picks = []
        for mask, flag in zip((low, high), is_high):
            picks.append(jnp.where(jnp.logical_xor(flag, mask == 1), band, 1 - band))
        flags = jnp.stack(picks + [flag.astype(jnp.int32) for flag in crossed])
        blocks = [
            pl.BlockSpec((1, 2, points, points), lambda s, f, n=n: (f[n], s, 0, 0))
            for n in (0, 0, 1, 1)
        ]
        sent = pl.pallas_call(
            pack_kernel,
            grid_spec=pltpu.PrefetchScalarGridSpec(
                num_scalar_prefetch=1,
                grid=(steps,),
                in_specs=blocks,
                out_specs=[pl.BlockSpec((2, points * 3 // 2, 128), lambda s, f: (s, 0, 0))] * 2,
            ),
            out_shape=[packed_shape] * 2,
            compiler_params=params,
        )(flags, values, other, values, other)
        branches = exchange_branches() + [same_chip(m) for m in chip_masks]
        return lax.switch(fetch_index, branches, *sent)

    def give_back(mirrors):
        sent = [jnp.where(c, swap(m, 1), m) for c, m in zip(crossed, mirrors)]
        total = (sent[0].astype(jnp.float32) + sent[1].astype(jnp.float32)).astype(jnp.bfloat16)
        first = jnp.where(one_chip, jnp.zeros_like(total), sent[0])
        second = jnp.where(one_chip, total, sent[1])
        return lax.switch(branch_index, exchange_branches(), first, second)

    def transform_in(band, partners):
        return pl.pallas_call(
            forward_kernel,
            grid=(steps,),
            in_specs=[
                band_spec(band, points),
                packed_spec(points),
                packed_spec(points),
                whole_spec(forward),
                whole_spec(plain),
            ],
            out_specs=pl.BlockSpec((points // 2, 2, 2, 2 * points), lambda s: (0, s, 0, 0)),
            out_shape=jax.ShapeDtypeStruct(
                (points // 2, slab_cells, 2, 2 * points), jnp.bfloat16
            ),
            compiler_params=params,
        )(bands, *partners, forward, plain)

    def send(values):
        return lax.all_to_all(values, "grid", split_axis=0, concat_axis=0, tiled=True)

    def screen_lines(received):
        block = (devices, 1, slab_cells, 2, 2 * points)
        return pl.pallas_call(
            screen_kernel,
            grid=(steps,),
            in_specs=[
                pl.BlockSpec(block, lambda s: (0, s, 0, 0, 0)),
                pl.BlockSpec((2,) + kernel_part.shape[1:], lambda s: (s, 0, 0)),
                whole_spec(gather),
                whole_spec(scatter),
            ],
            out_specs=pl.BlockSpec((points, 1, 2, 2 * points), lambda s: (0, s, 0, 0)),
            out_shape=jax.ShapeDtypeStruct((points, steps, 2, 2 * points), jnp.bfloat16),
            compiler_params=params,
        )(
            received.reshape(devices, steps, slab_cells, 2, 2 * points),
            kernel_part,
            gather,
            scatter,
        )

    def finish(band, partners, received):
        block = (devices, 2, steps, 2, 2 * points)
        return pl.pallas_call(
            lambda *refs: backward_kernel(factor, *refs),
            grid=(steps,),
            in_specs=[
                pl.BlockSpec(block, lambda s: (0, s, 0, 0, 0)),
                band_spec(band, points),
                packed_spec(points),
                packed_spec(points),
                whole_spec(single),
                whole_spec(backward),
            ],
            out_specs=[planes_spec(points)] + [packed_spec(points)] * 2,
            out_shape=[
                jax.ShapeDtypeStruct((slab_cells, points, points), jnp.float32),
                packed_shape,
                packed_shape,
            ],
            compiler_params=params,
        )(
            received.reshape(devices, slab_cells, steps, 2, 2 * points),
            bands,
            *partners,
            single,
            backward,
        )

    def combine(own_a, own_b, got_a, got_b):
        flags = jnp.stack(is_high).astype(jnp.int32)
        return pl.pallas_call(
            combine_kernel,
            grid=(steps,),
            in_specs=[pl.BlockSpec(memory_space=pltpu.SMEM)]
            + [planes_spec(points)] * 2
            + [packed_spec(points)] * 4,
            out_specs=pl.BlockSpec((2, 2, points, points), lambda s: (0, s, 0, 0)),
            out_shape=jax.ShapeDtypeStruct(bands.shape, jnp.float32),
            compiler_params=params,
        )(flags, own_a, own_b, *got_a, *got_b)

    together = lax.optimization_barrier
    partners_a = fetch(bands, sibling, 0)
    planes_a, bands_b, sibling_b = together((transform_in(0, partners_a), bands, sibling))
    lines_a = send(planes_a)
    partners_b = fetch(bands_b, sibling_b, 1)
    lines_a, planes_b = together((lines_a, transform_in(1, partners_b)))
    lines_b = send(planes_b)
    lines_b, screened_a = together((lines_b, screen_lines(lines_a)))
    back_a = send(screened_a)
    back_a, screened_b = together((back_a, screen_lines(lines_b)))
    back_b = send(screened_b)
    own_a, *mirrors_a = finish(0, partners_a, back_a)
    got_a = give_back(mirrors_a)
    back_b, own_a, got_a = together((back_b, own_a, got_a))
    own_b, *mirrors_b = finish(1, partners_b, back_b)
    got_b = give_back(mirrors_b)
    return combine(own_a, own_b, got_a, got_b)


def solution(mesh):
    in_specs = (P("band", "grid", None, None), P())
    out_specs = P("band", "grid", None, None)
    return jax.shard_map(
        per_device, mesh=mesh, in_specs=in_specs, out_specs=out_specs, check_vma=False
    )
```

```python
import math

import jax
import jax.numpy as jnp
import numpy as np
from jax import lax
from jax.experimental import pallas as pl
from jax.experimental.pallas import tpu as pltpu
from jax.sharding import PartitionSpec as P

screening = 0.11
cell_edge = 46.9
mixing = 0.25
decay = (2.0 * math.pi / cell_edge) ** 2 / (4.0 * screening**2)


def folded(index_values, points):
    return jnp.where(index_values < points // 2, index_values, index_values - points)


def kernel_values(freq_x, freq_y, freq_z):
    squares = freq_x * freq_x + freq_y * freq_y + freq_z * freq_z
    scaled = squares.astype(jnp.float32) * jnp.float32(decay)
    safe_value = jnp.where(squares == 0, jnp.float32(1.0), scaled)
    return jnp.where(squares == 0, jnp.float32(1.0), (1.0 - jnp.exp(-safe_value)) / safe_value)


def host_factor(points):
    index_values = np.arange(points)
    freq = np.where(index_values < points // 2, index_values, index_values - points)
    sq = freq * freq
    squares = sq[:, None, None] + sq[None, :, None] + sq[None, None, :]
    values, counts = np.unique(squares, return_counts=True)
    scaled = np.where(values == 0, 1.0, values * decay)
    kernel = np.where(values == 0, 1.0, -np.expm1(-scaled) / scaled)
    power = float(np.sum(kernel * kernel * counts))
    return 1.0 / math.sqrt(power / points**3) / points**3


def host_tables(points):
    index_values = np.arange(points)
    product = index_values[:, None] * index_values[None, :] % points
    angles = product.astype(np.float64) * (2.0 * math.pi / points)
    return np.cos(angles).astype(jnp.bfloat16), np.sin(angles).astype(jnp.bfloat16)


def lane_order(points):
    whole = points // 128 * 128
    real, imag = np.arange(points), points + np.arange(points)
    return np.concatenate([real[:whole], imag[:whole], real[whole:], imag[whole:]])


def device_tables(points, slab):
    cos_np, sin_np = host_tables(points)
    order = lane_order(points)
    forward = np.concatenate(
        [np.concatenate([cos_np, -sin_np], 1), np.concatenate([sin_np, cos_np], 1)], 0
    )[:, order]
    backward = np.concatenate(
        [np.concatenate([cos_np, sin_np], 1), np.concatenate([-sin_np, cos_np], 1)], 0
    )[order]
    lines = np.arange(points).reshape(points // slab, slab // 2, 2).transpose(1, 0, 2).reshape(-1)
    single = [t[:, lines] for t in (cos_np, sin_np)]
    eye = np.eye(2, dtype=cos_np.dtype)
    slabs = np.arange(points).reshape(points // slab, slab).transpose(1, 0).reshape(-1)
    gather = [
        (t[:, slabs][None, :, :, None] * eye[:, None, None, :]).reshape(2 * points, 2 * points)
        for t in (cos_np, sin_np)
    ]
    scatter = [
        (t[:, None, None, :] * eye[None, :, :, None]).reshape(2 * points, 2 * points)
        for t in (cos_np, sin_np)
    ]
    plain = [cos_np, sin_np]
    tables = [np.concatenate(t) for t in (plain, single, gather, scatter)]
    return [forward, backward] + tables


def matmul(left, right):
    return jnp.dot(left, right, preferred_element_type=jnp.float32)


def spin(tables, values, direction):
    rows = tables.shape[0] // 2
    both = matmul(tables[...], values)
    with_cos, with_sin = both[:rows], both[rows:]
    whole = values.shape[1] // 256 * 128
    rest = values.shape[1] - 2 * whole
    real = with_cos[:, :whole] + direction * with_sin[:, whole : 2 * whole]
    imag = with_cos[:, whole : 2 * whole] - direction * with_sin[:, :whole]
    turned = pltpu.roll(with_sin[:, 2 * whole :], rest // 2, 1)
    lanes = lax.broadcasted_iota(jnp.int32, turned.shape, 1)
    turned = jnp.where(lanes < rest // 2, direction * turned, -direction * turned)
    return real, imag, with_cos[:, 2 * whole :] + turned


def joined(parts):
    return jnp.concatenate([part.astype(jnp.bfloat16) for part in parts], axis=1)


def packed(plane):
    whole = plane.shape[1] // 128 * 128
    half = plane.shape[0] // 2
    rest = jnp.concatenate([plane[:half, whole:], plane[half:, whole:]], axis=1)
    return jnp.concatenate([plane[:, :whole], rest], axis=0)


def unpacked(plane):
    rows = plane.shape[0] * 2 // 3
    half = plane.shape[1] // 2
    rest = jnp.concatenate([plane[rows:, :half], plane[rows:, half:]], axis=0)
    return jnp.concatenate([plane[:rows], rest], axis=1)


def pack_kernel(flags, own_low, other_low, own_high, other_high, low, high):
    for n, (own, other, out) in enumerate(
        ((own_low, other_low, low), (own_high, other_high, high))
    ):
        for member in range(out.shape[0]):
            mine = own[0, member].astype(jnp.float32)
            theirs = other[0, member].astype(jnp.float32)
            plane = jnp.where(flags[2 + n] == 1, theirs, mine)
            out[member] = packed(plane).astype(jnp.bfloat16)


def forward_kernel(own, low, high, forward, plain, out):
    points = own.shape[-1]
    members = range(own.shape[1])

    def density(partner):
        planes = []
        for n in members:
            theirs = unpacked(partner[n].astype(jnp.float32))
            planes.append((own[0, n].astype(jnp.float32) * theirs).astype(jnp.bfloat16))
        return jnp.concatenate(planes, axis=0)

    first = matmul(density(low), forward[:points]) + matmul(density(high), forward[points:])
    first = first.astype(jnp.bfloat16)
    for n in members:
        spectrum = joined(spin(plain, first[n * points : (n + 1) * points], 1.0))
        out[:, n] = spectrum.reshape(points // 2, 2, 2 * points)


def screen_kernel(lines, kernel, gather, scatter, out):
    points = out.shape[0]
    whole = points // 128 * 128
    gathered = jnp.concatenate(
        [lines[:, 0, plane].reshape(-1, 2 * points) for plane in range(lines.shape[2])], 0
    )
    real, imag, rest = spin(gather, gathered, 1.0)
    near = kernel[:, :, :whole].reshape(2 * points, whole)
    far = kernel[:, :, whole:].reshape(2 * points, whole)
    screened = joined([real * near, imag * near, rest * far])
    back = joined(spin(scatter, screened, -1.0))
    out[:, 0] = back.reshape(points, 2, 2 * points)


def backward_kernel(factor, lines, band, low, high, single, backward, own, to_low, to_high):
    points = band.shape[-1]
    members = range(band.shape[1])
    backs = []
    for n in members:
        gathered = jnp.concatenate(
            [lines[:, n, pair].reshape(-1, 2 * points) for pair in range(lines.shape[2])], 0
        )
        backs.append(joined(spin(single, gathered, -1.0)))
    back = jnp.concatenate(backs, axis=0)
    potentials = [
        matmul(back, backward[:, start : start + points]) * factor for start in (0, points)
    ]
    for n in members:
        mine = band[0, n].astype(jnp.float32)
        total = jnp.zeros((points, points), jnp.float32)
        for potential, partner, mirror in zip(potentials, (low, high), (to_low, to_high)):
            here = potential[n * points : (n + 1) * points]
            mirror[n] = packed(here * mine).astype(jnp.bfloat16)
            total = total + here * unpacked(partner[n].astype(jnp.float32))
        own[n] = -mixing * total


def combine_kernel(flags, own_a, own_b, a_low, a_high, b_low, b_high, out):
    for member in range(own_a.shape[0]):
        for target, own in enumerate((own_a, own_b)):
            got = 0.0
            for n, (from_a, from_b) in enumerate(((a_low, b_low), (a_high, b_high))):
                kept = flags[n] == 1 - target
                mine, theirs = from_a[member], from_b[member]
                got = got + jnp.where(kept, mine.astype(jnp.float32), theirs.astype(jnp.float32))
            out[target, member] = own[member] - mixing * unpacked(got)


def whole_spec(array):
    rank = len(array.shape)
    return pl.BlockSpec(array.shape, lambda s: (0,) * rank)


def planes_spec(points, count=2):
    return pl.BlockSpec((count, points, points), lambda s: (s, 0, 0))


def packed_spec(points, count=2):
    return pl.BlockSpec((count, points * 3 // 2, 128), lambda s: (s, 0, 0))


def band_spec(band, points):
    return pl.BlockSpec((1, 2, points, points), lambda s: (band, s, 0, 0))


params = pltpu.CompilerParams(vmem_limit_bytes=32 * 1024 * 1024)


def per_device(bands, plan):
    slab_cells = bands.shape[1]
    points = bands.shape[2]
    band_count = lax.axis_size("band")
    my_block = lax.axis_index("band")
    forward, backward, plain, single, gather, scatter = [
        jnp.asarray(table) for table in device_tables(points, slab_cells)
    ]
    steps = slab_cells // 2
    devices = points // slab_cells
    packed_shape = jax.ShapeDtypeStruct((slab_cells, points * 3 // 2, 128), jnp.bfloat16)
    factor = host_factor(points)
    frequency = folded(jnp.arange(points, dtype=jnp.int32), points)
    column_ids = lax.axis_index("grid") * slab_cells + jnp.arange(slab_cells, dtype=jnp.int32)
    kernel_part = kernel_values(
        folded(column_ids, points)[:, None, None],
        frequency[None, :, None],
        jnp.concatenate([frequency, frequency[points // 128 * 128 :]])[None, None, :],
    )

    def swap(values, mask):
        return lax.ppermute(values, "band", [(i, i ^ mask) for i in range(band_count)])

    low = jnp.minimum(plan[0, 0], plan[1, 0])
    high = jnp.maximum(plan[0, 0], plan[1, 0])
    chip_low, chip_high = low // 2, high // 2
    chip_masks = range(1, band_count // 2)
    one_chip = chip_low == chip_high
    lone = jnp.logical_or(chip_low == 0, one_chip)
    pairs = [(i, j) for i in chip_masks for j in chip_masks if i < j]
    pair_index = sum(
        jnp.where(jnp.logical_and(chip_low == i, chip_high == j), n + len(chip_masks), 0)
        for n, (i, j) in enumerate(pairs)
    )
    branch_index = jnp.where(lone, chip_high - 1, pair_index)
    fetch_index = jnp.where(one_chip, chip_high - 1 + len(chip_masks) + len(pairs), branch_index)
    is_high = [my_block > jnp.bitwise_xor(my_block, mask) for mask in (low, high)]
    crossed = [mask % 2 == 1 for mask in (low, high)]

    def exchange_branches():
        singles = [lambda u, v, m=m: (u, swap(v, 2 * m)) for m in chip_masks]
        doubles = [lambda u, v, m=m: (swap(u, 2 * m[0]), swap(v, 2 * m[1])) for m in pairs]
        return singles + doubles

    def same_chip(mask):
        def branch(u, v):
            got = swap(v, 2 * mask)
            return swap(got, 1), got

        return branch

    def merged_chip(mask):
        def branch(u, v):
            total = u.astype(jnp.float32) + v.astype(jnp.float32)
            return jnp.zeros_like(u), swap(total.astype(u.dtype), 2 * mask)

        return branch

    sibling = swap(bands, 1)

    def fetch(values, other, band):
        picks = []
        for mask, flag in zip((low, high), is_high):
            picks.append(jnp.where(jnp.logical_xor(flag, mask == 1), band, 1 - band))
        flags = jnp.stack(picks + [flag.astype(jnp.int32) for flag in crossed])
        blocks = [
            pl.BlockSpec((1, 2, points, points), lambda s, f, n=n: (f[n], s, 0, 0))
            for n in (0, 0, 1, 1)
        ]
        sent = pl.pallas_call(
            pack_kernel,
            grid_spec=pltpu.PrefetchScalarGridSpec(
                num_scalar_prefetch=1,
                grid=(steps,),
                in_specs=blocks,
                out_specs=[pl.BlockSpec((2, points * 3 // 2, 128), lambda s, f: (s, 0, 0))] * 2,
            ),
            out_shape=[packed_shape] * 2,
            compiler_params=params,
        )(flags, values, other, values, other)
        branches = exchange_branches() + [same_chip(m) for m in chip_masks]
        return lax.switch(fetch_index, branches, *sent)

    def give_back(mirrors):
        sent = [jnp.where(c, swap(m, 1), m) for c, m in zip(crossed, mirrors)]
        branches = exchange_branches() + [merged_chip(m) for m in chip_masks]
        return lax.switch(fetch_index, branches, *sent)

    def transform_in(band, partners):
        return pl.pallas_call(
            forward_kernel,
            grid=(steps,),
            in_specs=[
                band_spec(band, points),
                packed_spec(points),
                packed_spec(points),
                whole_spec(forward),
                whole_spec(plain),
            ],
            out_specs=pl.BlockSpec((points // 2, 2, 2, 2 * points), lambda s: (0, s, 0, 0)),
            out_shape=jax.ShapeDtypeStruct(
                (points // 2, slab_cells, 2, 2 * points), jnp.bfloat16
            ),
            compiler_params=params,
        )(bands, *partners, forward, plain)

    def send(values):
        return lax.all_to_all(values, "grid", split_axis=0, concat_axis=0, tiled=True)

    def screen_lines(received):
        block = (devices, 1, slab_cells, 2, 2 * points)
        return pl.pallas_call(
            screen_kernel,
            grid=(steps,),
            in_specs=[
                pl.BlockSpec(block, lambda s: (0, s, 0, 0, 0)),
                pl.BlockSpec((2,) + kernel_part.shape[1:], lambda s: (s, 0, 0)),
                whole_spec(gather),
                whole_spec(scatter),
            ],
            out_specs=pl.BlockSpec((points, 1, 2, 2 * points), lambda s: (0, s, 0, 0)),
            out_shape=jax.ShapeDtypeStruct((points, steps, 2, 2 * points), jnp.bfloat16),
            compiler_params=params,
        )(
            received.reshape(devices, steps, slab_cells, 2, 2 * points),
            kernel_part,
            gather,
            scatter,
        )

    def finish(band, partners, received):
        block = (devices, 2, steps, 2, 2 * points)
        return pl.pallas_call(
            lambda *refs: backward_kernel(factor, *refs),
            grid=(steps,),
            in_specs=[
                pl.BlockSpec(block, lambda s: (0, s, 0, 0, 0)),
                band_spec(band, points),
                packed_spec(points),
                packed_spec(points),
                whole_spec(single),
                whole_spec(backward),
            ],
            out_specs=[planes_spec(points)] + [packed_spec(points)] * 2,
            out_shape=[
                jax.ShapeDtypeStruct((slab_cells, points, points), jnp.float32),
                packed_shape,
                packed_shape,
            ],
            compiler_params=params,
        )(
            received.reshape(devices, slab_cells, steps, 2, 2 * points),
            bands,
            *partners,
            single,
            backward,
        )

    def combine(own_a, own_b, got_a, got_b):
        flags = jnp.stack(is_high).astype(jnp.int32)
        return pl.pallas_call(
            combine_kernel,
            grid=(steps,),
            in_specs=[pl.BlockSpec(memory_space=pltpu.SMEM)]
            + [planes_spec(points)] * 2
            + [packed_spec(points)] * 4,
            out_specs=pl.BlockSpec((2, 2, points, points), lambda s: (0, s, 0, 0)),
            out_shape=jax.ShapeDtypeStruct(bands.shape, jnp.float32),
            compiler_params=params,
        )(flags, own_a, own_b, *got_a, *got_b)

    together = lax.optimization_barrier
    partners_a = fetch(bands, sibling, 0)
    planes_a, bands_b, sibling_b = together((transform_in(0, partners_a), bands, sibling))
    lines_a = send(planes_a)
    partners_b = fetch(bands_b, sibling_b, 1)
    lines_a, planes_b = together((lines_a, transform_in(1, partners_b)))
    lines_b = send(planes_b)
    lines_b, screened_a = together((lines_b, screen_lines(lines_a)))
    back_a = send(screened_a)
    back_a, screened_b = together((back_a, screen_lines(lines_b)))
    back_b = send(screened_b)
    own_a, *mirrors_a = finish(0, partners_a, back_a)
    got_a = give_back(mirrors_a)
    back_b, own_a, got_a = together((back_b, own_a, got_a))
    own_b, *mirrors_b = finish(1, partners_b, back_b)
    got_b = give_back(mirrors_b)
    return combine(own_a, own_b, got_a, got_b)


def solution(mesh):
    in_specs = (P("band", "grid", None, None), P())
    out_specs = P("band", "grid", None, None)
    return jax.shard_map(
        per_device, mesh=mesh, in_specs=in_specs, out_specs=out_specs, check_vma=False
    )
```

```python
import math

import jax
import jax.numpy as jnp
import numpy as np
from jax import lax
from jax.experimental import pallas as pl
from jax.experimental.pallas import tpu as pltpu
from jax.sharding import PartitionSpec as P

screening = 0.11
cell_edge = 46.9
mixing = 0.25
decay = (2.0 * math.pi / cell_edge) ** 2 / (4.0 * screening**2)


def folded(index_values, points):
    return jnp.where(index_values < points // 2, index_values, index_values - points)


def kernel_values(freq_x, freq_y, freq_z):
    squares = freq_x * freq_x + freq_y * freq_y + freq_z * freq_z
    scaled = squares.astype(jnp.float32) * jnp.float32(decay)
    safe_value = jnp.where(squares == 0, jnp.float32(1.0), scaled)
    return jnp.where(squares == 0, jnp.float32(1.0), (1.0 - jnp.exp(-safe_value)) / safe_value)


def host_factor(points):
    index_values = np.arange(points)
    freq = np.where(index_values < points // 2, index_values, index_values - points)
    sq = freq * freq
    squares = sq[:, None, None] + sq[None, :, None] + sq[None, None, :]
    values, counts = np.unique(squares, return_counts=True)
    scaled = np.where(values == 0, 1.0, values * decay)
    kernel = np.where(values == 0, 1.0, -np.expm1(-scaled) / scaled)
    power = float(np.sum(kernel * kernel * counts))
    return 1.0 / math.sqrt(power / points**3) / points**3


def host_tables(points):
    index_values = np.arange(points)
    product = index_values[:, None] * index_values[None, :] % points
    angles = product.astype(np.float64) * (2.0 * math.pi / points)
    return np.cos(angles).astype(jnp.bfloat16), np.sin(angles).astype(jnp.bfloat16)


def lane_order(points):
    whole = points // 128 * 128
    real, imag = np.arange(points), points + np.arange(points)
    return np.concatenate([real[:whole], imag[:whole], real[whole:], imag[whole:]])


def device_tables(points, slab):
    cos_np, sin_np = host_tables(points)
    order = lane_order(points)
    forward = np.concatenate(
        [np.concatenate([cos_np, -sin_np], 1), np.concatenate([sin_np, cos_np], 1)], 0
    )[:, order]
    backward = np.concatenate(
        [np.concatenate([cos_np, sin_np], 1), np.concatenate([-sin_np, cos_np], 1)], 0
    )[order]
    lines = np.arange(points).reshape(points // slab, slab // 2, 2).transpose(1, 0, 2).reshape(-1)
    single = [t[:, lines] for t in (cos_np, sin_np)]
    eye = np.eye(2, dtype=cos_np.dtype)
    slabs = np.arange(points).reshape(points // slab, slab).transpose(1, 0).reshape(-1)
    gather = [
        (t[:, slabs][None, :, :, None] * eye[:, None, None, :]).reshape(2 * points, 2 * points)
        for t in (cos_np, sin_np)
    ]
    scatter = [
        (t[:, None, None, :] * eye[None, :, :, None]).reshape(2 * points, 2 * points)
        for t in (cos_np, sin_np)
    ]
    plain = [cos_np, sin_np]
    tables = [np.concatenate(t) for t in (plain, single, gather, scatter)]
    return [forward, backward] + tables


def matmul(left, right):
    return jnp.dot(left, right, preferred_element_type=jnp.float32)


def spin(tables, values, direction):
    rows = tables.shape[0] // 2
    both = matmul(tables[...], values)
    with_cos, with_sin = both[:rows], both[rows:]
    whole = values.shape[1] // 256 * 128
    rest = values.shape[1] - 2 * whole
    real = with_cos[:, :whole] + direction * with_sin[:, whole : 2 * whole]
    imag = with_cos[:, whole : 2 * whole] - direction * with_sin[:, :whole]
    turned = pltpu.roll(with_sin[:, 2 * whole :], rest // 2, 1)
    lanes = lax.broadcasted_iota(jnp.int32, turned.shape, 1)
    turned = jnp.where(lanes < rest // 2, direction * turned, -direction * turned)
    return real, imag, with_cos[:, 2 * whole :] + turned


def joined(parts):
    return jnp.concatenate([part.astype(jnp.bfloat16) for part in parts], axis=1)


def packed(plane):
    whole = plane.shape[1] // 128 * 128
    half = plane.shape[0] // 2
    rest = jnp.concatenate([plane[:half, whole:], plane[half:, whole:]], axis=1)
    return jnp.concatenate([plane[:, :whole], rest], axis=0)


def unpacked(plane):
    rows = plane.shape[0] * 2 // 3
    half = plane.shape[1] // 2
    rest = jnp.concatenate([plane[rows:, :half], plane[rows:, half:]], axis=0)
    return jnp.concatenate([plane[:rows], rest], axis=1)


def pack_kernel(flags, own_low, other_low, own_high, other_high, low, high):
    for n, (own, other, out) in enumerate(
        ((own_low, other_low, low), (own_high, other_high, high))
    ):
        for member in range(out.shape[0]):
            plane = jnp.where(flags[2 + n] == 1, other[0, member], own[0, member])
            out[member] = packed(plane.astype(jnp.float32)).astype(jnp.bfloat16)


def forward_kernel(own, low, high, forward, plain, out):
    points = own.shape[-1]
    members = range(own.shape[1])

    def density(partner):
        planes = []
        for n in members:
            theirs = unpacked(partner[n].astype(jnp.float32))
            planes.append((own[0, n].astype(jnp.float32) * theirs).astype(jnp.bfloat16))
        return jnp.concatenate(planes, axis=0)

    first = matmul(density(low), forward[:points]) + matmul(density(high), forward[points:])
    first = first.astype(jnp.bfloat16)
    for n in members:
        spectrum = joined(spin(plain, first[n * points : (n + 1) * points], 1.0))
        out[:, n] = spectrum.reshape(points // 2, 2, 2 * points)


def screen_kernel(lines, kernel, gather, scatter, out):
    points = out.shape[0]
    whole = points // 128 * 128
    gathered = jnp.concatenate(
        [lines[:, 0, plane].reshape(-1, 2 * points) for plane in range(lines.shape[2])], 0
    )
    real, imag, rest = spin(gather, gathered, 1.0)
    near = kernel[:, :, :whole].reshape(2 * points, whole)
    far = kernel[:, :, whole:].reshape(2 * points, whole)
    screened = joined([real * near, imag * near, rest * far])
    back = joined(spin(scatter, screened, -1.0))
    out[:, 0] = back.reshape(points, 2, 2 * points)


def backward_kernel(factor, lines, band, low, high, single, backward, own, to_low, to_high):
    points = band.shape[-1]
    members = range(band.shape[1])
    backs = []
    for n in members:
        gathered = jnp.concatenate(
            [lines[:, n, pair].reshape(-1, 2 * points) for pair in range(lines.shape[2])], 0
        )
        backs.append(joined(spin(single, gathered, -1.0)))
    back = jnp.concatenate(backs, axis=0)
    potentials = [
        matmul(back, backward[:, start : start + points]) * factor for start in (0, points)
    ]
    for n in members:
        mine = band[0, n].astype(jnp.float32)
        total = jnp.zeros((points, points), jnp.float32)
        for potential, partner, mirror in zip(potentials, (low, high), (to_low, to_high)):
            here = potential[n * points : (n + 1) * points]
            mirror[n] = packed(here * mine).astype(jnp.bfloat16)
            total = total + here * unpacked(partner[n].astype(jnp.float32))
        own[n] = -mixing * total


def combine_kernel(flags, own_a, own_b, a_low, a_high, b_low, b_high, out):
    for member in range(own_a.shape[0]):
        for target, own in enumerate((own_a, own_b)):
            got = 0.0
            for n, (from_a, from_b) in enumerate(((a_low, b_low), (a_high, b_high))):
                kept = flags[n] == 1 - target
                got = got + jnp.where(kept, from_a[member], from_b[member]).astype(jnp.float32)
            out[target, member] = own[member] - mixing * unpacked(got)


def whole_spec(array):
    rank = len(array.shape)
    return pl.BlockSpec(array.shape, lambda s: (0,) * rank)


def planes_spec(points, count=2):
    return pl.BlockSpec((count, points, points), lambda s: (s, 0, 0))


def packed_spec(points, count=2):
    return pl.BlockSpec((count, points * 3 // 2, 128), lambda s: (s, 0, 0))


def band_spec(band, points):
    return pl.BlockSpec((1, 2, points, points), lambda s: (band, s, 0, 0))


params = pltpu.CompilerParams(vmem_limit_bytes=32 * 1024 * 1024)


def per_device(bands, plan):
    slab_cells = bands.shape[1]
    points = bands.shape[2]
    band_count = lax.axis_size("band")
    my_block = lax.axis_index("band")
    forward, backward, plain, single, gather, scatter = [
        jnp.asarray(table) for table in device_tables(points, slab_cells)
    ]
    steps = slab_cells // 2
    devices = points // slab_cells
    packed_shape = jax.ShapeDtypeStruct((slab_cells, points * 3 // 2, 128), jnp.bfloat16)
    factor = host_factor(points)
    frequency = folded(jnp.arange(points, dtype=jnp.int32), points)
    column_ids = lax.axis_index("grid") * slab_cells + jnp.arange(slab_cells, dtype=jnp.int32)
    kernel_part = kernel_values(
        folded(column_ids, points)[:, None, None],
        frequency[None, :, None],
        jnp.concatenate([frequency, frequency[points // 128 * 128 :]])[None, None, :],
    )

    def swap(values, mask):
        return lax.ppermute(values, "band", [(i, i ^ mask) for i in range(band_count)])

    low = jnp.minimum(plan[0, 0], plan[1, 0])
    high = jnp.maximum(plan[0, 0], plan[1, 0])
    chip_low, chip_high = low // 2, high // 2
    chip_masks = range(1, band_count // 2)
    one_chip = chip_low == chip_high
    lone = jnp.logical_or(chip_low == 0, one_chip)
    pairs = [(i, j) for i in chip_masks for j in chip_masks if i < j]
    pair_index = sum(
        jnp.where(jnp.logical_and(chip_low == i, chip_high == j), n + len(chip_masks), 0)
        for n, (i, j) in enumerate(pairs)
    )
    branch_index = jnp.where(lone, chip_high - 1, pair_index)
    fetch_index = jnp.where(one_chip, chip_high - 1 + len(chip_masks) + len(pairs), branch_index)
    is_high = [my_block > jnp.bitwise_xor(my_block, mask) for mask in (low, high)]
    crossed = [mask % 2 == 1 for mask in (low, high)]

    def exchange_branches():
        singles = [lambda u, v, m=m: (u, swap(v, 2 * m)) for m in chip_masks]
        doubles = [lambda u, v, m=m: (swap(u, 2 * m[0]), swap(v, 2 * m[1])) for m in pairs]
        return singles + doubles

    def same_chip(mask):
        def branch(u, v):
            got = swap(v, 2 * mask)
            return swap(got, 1), got

        return branch

    def merged_chip(mask):
        def branch(u, v):
            total = u.astype(jnp.float32) + v.astype(jnp.float32)
            return jnp.zeros_like(u), swap(total.astype(u.dtype), 2 * mask)

        return branch

    sibling = swap(bands, 1)

    def fetch(values, other, band):
        picks = []
        for mask, flag in zip((low, high), is_high):
            picks.append(jnp.where(jnp.logical_xor(flag, mask == 1), band, 1 - band))
        flags = jnp.stack(picks + [flag.astype(jnp.int32) for flag in crossed])
        blocks = [
            pl.BlockSpec((1, 2, points, points), lambda s, f, n=n: (f[n], s, 0, 0))
            for n in (0, 0, 1, 1)
        ]
        sent = pl.pallas_call(
            pack_kernel,
            grid_spec=pltpu.PrefetchScalarGridSpec(
                num_scalar_prefetch=1,
                grid=(steps,),
                in_specs=blocks,
                out_specs=[pl.BlockSpec((2, points * 3 // 2, 128), lambda s, f: (s, 0, 0))] * 2,
            ),
            out_shape=[packed_shape] * 2,
            compiler_params=params,
        )(flags, values, other, values, other)
        branches = exchange_branches() + [same_chip(m) for m in chip_masks]
        return lax.switch(fetch_index, branches, *sent)

    def give_back(mirrors):
        sent = [jnp.where(c, swap(m, 1), m) for c, m in zip(crossed, mirrors)]
        branches = exchange_branches() + [merged_chip(m) for m in chip_masks]
        return lax.switch(fetch_index, branches, *sent)

    def transform_in(band, partners):
        return pl.pallas_call(
            forward_kernel,
            grid=(steps,),
            in_specs=[
                band_spec(band, points),
                packed_spec(points),
                packed_spec(points),
                whole_spec(forward),
                whole_spec(plain),
            ],
            out_specs=pl.BlockSpec((points // 2, 2, 2, 2 * points), lambda s: (0, s, 0, 0)),
            out_shape=jax.ShapeDtypeStruct(
                (points // 2, slab_cells, 2, 2 * points), jnp.bfloat16
            ),
            compiler_params=params,
        )(bands, *partners, forward, plain)

    def send(values):
        return lax.all_to_all(values, "grid", split_axis=0, concat_axis=0, tiled=True)

    def screen_lines(received):
        block = (devices, 1, slab_cells, 2, 2 * points)
        return pl.pallas_call(
            screen_kernel,
            grid=(steps,),
            in_specs=[
                pl.BlockSpec(block, lambda s: (0, s, 0, 0, 0)),
                pl.BlockSpec((2,) + kernel_part.shape[1:], lambda s: (s, 0, 0)),
                whole_spec(gather),
                whole_spec(scatter),
            ],
            out_specs=pl.BlockSpec((points, 1, 2, 2 * points), lambda s: (0, s, 0, 0)),
            out_shape=jax.ShapeDtypeStruct((points, steps, 2, 2 * points), jnp.bfloat16),
            compiler_params=params,
        )(
            received.reshape(devices, steps, slab_cells, 2, 2 * points),
            kernel_part,
            gather,
            scatter,
        )

    def finish(band, partners, received):
        block = (devices, 2, steps, 2, 2 * points)
        return pl.pallas_call(
            lambda *refs: backward_kernel(factor, *refs),
            grid=(steps,),
            in_specs=[
                pl.BlockSpec(block, lambda s: (0, s, 0, 0, 0)),
                band_spec(band, points),
                packed_spec(points),
                packed_spec(points),
                whole_spec(single),
                whole_spec(backward),
            ],
            out_specs=[planes_spec(points)] + [packed_spec(points)] * 2,
            out_shape=[
                jax.ShapeDtypeStruct((slab_cells, points, points), jnp.float32),
                packed_shape,
                packed_shape,
            ],
            compiler_params=params,
        )(
            received.reshape(devices, slab_cells, steps, 2, 2 * points),
            bands,
            *partners,
            single,
            backward,
        )

    def combine(own_a, own_b, got_a, got_b):
        flags = jnp.stack(is_high).astype(jnp.int32)
        return pl.pallas_call(
            combine_kernel,
            grid=(steps,),
            in_specs=[pl.BlockSpec(memory_space=pltpu.SMEM)]
            + [planes_spec(points)] * 2
            + [packed_spec(points)] * 4,
            out_specs=pl.BlockSpec((2, 2, points, points), lambda s: (0, s, 0, 0)),
            out_shape=jax.ShapeDtypeStruct(bands.shape, jnp.float32),
            compiler_params=params,
        )(flags, own_a, own_b, *got_a, *got_b)

    together = lax.optimization_barrier
    partners_a = fetch(bands, sibling, 0)
    planes_a, bands_b, sibling_b = together((transform_in(0, partners_a), bands, sibling))
    lines_a = send(planes_a)
    partners_b = fetch(bands_b, sibling_b, 1)
    lines_a, planes_b = together((lines_a, transform_in(1, partners_b)))
    lines_b = send(planes_b)
    lines_b, screened_a = together((lines_b, screen_lines(lines_a)))
    back_a = send(screened_a)
    back_a, screened_b = together((back_a, screen_lines(lines_b)))
    back_b = send(screened_b)
    own_a, *mirrors_a = finish(0, partners_a, back_a)
    got_a = give_back(mirrors_a)
    back_b, own_a, got_a = together((back_b, own_a, got_a))
    own_b, *mirrors_b = finish(1, partners_b, back_b)
    got_b = give_back(mirrors_b)
    return combine(own_a, own_b, got_a, got_b)


def solution(mesh):
    in_specs = (P("band", "grid", None, None), P())
    out_specs = P("band", "grid", None, None)
    return jax.shard_map(
        per_device, mesh=mesh, in_specs=in_specs, out_specs=out_specs, check_vma=False
    )
```
